128 devices in a mesh: rep: 8 (over x, z_hi), tp: 16 (over z_lo, y, core).
Axes of the slice: x: 4, y: 4, z: 4 (z_hi: 2, z_lo: 2; z = z_hi * 2 + z_lo), core: 2. Of those that a mesh axis runs over, the one named last changes fastest.
Arguments:
- hidden_in: bfloat16 [8192, 8192], P('rep'), may hold values from -6 to 6
- norm_gain: float32 [8192], replicated, may hold values from 0.1 to 1.9
- w_query: bfloat16 [8192, 8192], P(('rep', 'tp'))
- w_keyval: bfloat16 [8192, 2048], P(('rep', 'tp'))
- w_out: bfloat16 [8192, 8192], P(None, ('rep', 'tp')), may hold values from -0.25 to 0.25
- doc_lengths: int32 [8, 4], P('rep'), may hold values from 1 to 512, 1024 in all within a row
Outputs:
- mixed: bfloat16 [8192, 8192], P(('rep', 'tp'))
The draws below stay inside these ranges and needn't reach their ends.
Inputs may be any that keep to these rules, and one draw needn't show every extreme that they name: `doc_lengths`: each replica's lengths sum to 1024, and the longest has exactly 512 tokens.
All inputs are finite; a program needn't handle non-finite values.
Results may differ from the reference program's by a relative error of at most 0.023.
The reference program's roundings to bfloat16 on the way count: a program that leaves them out, or rounds other values in their place, can miss the bound.
Values may be sent and summed in bfloat16 or wider, within the bound.
No kernel may reach another device: no remote copies, remote signals or barrier semaphores. Data moves between devices by JAX's collectives and lax.ppermute only.
A program may use at most 192 MiB of HBM per device.

```python
import math
import jax
import jax.numpy as jnp
import numpy as np
from jax import lax

D = 8192
H = 64
KVH = 8
HD = 128
SEQ = 1024
NDOC = 4
REPS = 8
TOKENS = 8192
N_TP = 16


def draw_w_query(key, part):
    key = jax.random.fold_in(key, 21)
    fresh = jax.random.normal(key, (D, H * HD), jnp.float32)
    return (fresh / math.sqrt(D)).astype(jnp.bfloat16)


def draw_w_keyval(key, part):
    key = jax.random.fold_in(key, 22)
    fresh = jax.random.normal(key, (D, 2 * KVH * HD), jnp.float32)
    return (fresh / math.sqrt(D)).astype(jnp.bfloat16)


def steps_of(stream_key, shape, shards, least, top_value):
    gain, own = 1.0, jax.random.fold_in(stream_key, 6)
    for axis_at, blocks in shards:
        heights = jnp.exp(jax.random.uniform(jax.random.fold_in(own, axis_at), (blocks,), jnp.float32, least / len(shards), top_value / len(shards)))
        gain = gain * jnp.repeat(heights, shape[axis_at] // blocks).reshape([-1 if axis == axis_at else 1 for axis in range(len(shape))])
    return gain


def split_up(count, total, bound, slope):
    portions = [(1 << 20) // math.isqrt(rank ** slope) + 1 for rank in range(2, count + 1)]
    rest, holding = total - bound - (count - 1), [1] * (count - 1)
    while rest > 0:
        candidates = [i for i in range(count - 1) if holding[i] < bound]
        mass, remaining = sum([portions[i] for i in candidates]), rest
        for i in candidates:
            more = min(bound - holding[i], max(1, remaining * portions[i] // mass), rest)
            holding[i] = holding[i] + more
            rest = rest - more
    return np.array([bound] + holding)


def uneven_parts(own_key, number_of, total, bound, slope):
    if number_of == 2:
        one = jax.random.randint(own_key, (), max(1, total - bound), min(bound, total - 1) + 1)
        return jnp.stack([one, total - one])
    tallies = jnp.asarray(split_up(number_of, total, bound, slope), jnp.int32)
    couples = (number_of - 1) // 2
    source_of, receiver = tallies[1:1 + 2 * couples:2], tallies[2:2 + 2 * couples:2]
    room = jnp.minimum(source_of - 1, bound - receiver)
    shifted = jax.random.randint(jax.random.fold_in(own_key, 1), (couples,), 0, 1 << 20) % (room + 1)
    tallies = tallies.at[1:1 + 2 * couples:2].set(source_of - shifted).at[2:2 + 2 * couples:2].set(receiver + shifted)
    return tallies[jax.random.permutation(jax.random.fold_in(own_key, 2), number_of)]


def noise(stream_key, extent, scale, reach, shards=(), kind=jnp.bfloat16):
    loudness = steps_of(stream_key, extent, shards, -0.22, 0.18) if shards else 1.0
    result = jax.random.normal(stream_key, extent, jnp.float32) * scale * loudness
    return jnp.minimum(jnp.maximum(result, -reach), reach).astype(kind)


def setup_inputs(seed: int = 0) -> dict:
    key_of = jax.random.split(jax.random.key(seed), 7)
    return {
        "hidden_in": noise(key_of[0], (TOKENS, D), 1.0, 6.0, ((0, 8),)),
        "norm_gain": jnp.clip(1.0 + 0.18 * jax.random.normal(key_of[1], (D,), jnp.float32), 0.1, 1.9),
        "w_query": draw_w_query(jax.random.fold_in(key_of[6], 71), 0),
        "w_keyval": draw_w_keyval(jax.random.fold_in(key_of[6], 71), 0),
        "w_out": noise(key_of[4], (H * HD, D), (H * HD // 16) ** -0.5, 0.25, ((1, 128),)),
        "doc_lengths": jax.vmap(lambda own: uneven_parts(own, NDOC, SEQ, SEQ // 2, 2))(jax.random.split(key_of[5], REPS)).reshape((REPS, NDOC)).astype(jnp.int32),
    }


theta_base = 1000000.0
eps_norm = 1e-06

def rotary(tensor, positions):
    half = tensor.shape[-1] // 2
    freqs = theta_base ** (-(jnp.arange(half, dtype=jnp.float32) * 2.0 / tensor.shape[-1]))
    angles = positions.astype(jnp.float32)[:, None] * freqs[None, :]
    cosine = jnp.cos(angles)[:, None, :]
    sine = jnp.sin(angles)[:, None, :]
    first = tensor[..., :half]
    second = tensor[..., half:]
    return jnp.concatenate([first * cosine - second * sine, second * cosine + first * sine], axis=-1)

def doc_layout(lengths, count):
    places = jnp.arange(count, dtype=jnp.int32)
    ends = jnp.cumsum(lengths).astype(jnp.int32)
    after = places[:, None] >= ends[None, :]
    segment = lax.optimization_barrier(jnp.sum(after.astype(jnp.int32), axis=1)).astype(jnp.int32)
    starts = lax.optimization_barrier(jnp.sum(jnp.where(after, lengths[None, :], 0), axis=1)).astype(jnp.int32)
    return (places, segment, places - starts)

def attend(query, keys, values, places, segment):
    count = query.shape[0]
    block = min(count, 512)
    scale = keys.shape[-1] ** (-0.5)

    def one_block(number):
        begin = number * block
        rows = lax.dynamic_slice_in_dim(query, begin, block, 0)
        row_place = lax.dynamic_slice_in_dim(places, begin, block, 0)
        row_seg = lax.dynamic_slice_in_dim(segment, begin, block, 0)
        scores = jnp.einsum('qgd,kd->gqk', rows.astype(jnp.float32), keys.astype(jnp.float32)) * scale
        allowed = (row_seg[:, None] == segment[None, :]) & (places[None, :] <= row_place[:, None])
        scores = jnp.where(allowed[None], scores, -1e+30)
        top = lax.optimization_barrier(jnp.max(scores, axis=-1, keepdims=True))
        weights = jnp.exp(scores - top)
        probs = (weights / lax.optimization_barrier(jnp.sum(weights, axis=-1, keepdims=True))).astype(jnp.bfloat16)
        blended = jnp.einsum('gqk,kd->qgd', probs.astype(jnp.float32), values.astype(jnp.float32))
        return blended.astype(jnp.bfloat16).reshape(block, -1)
    numbers = jnp.arange(count // block, dtype=jnp.int32)
    return lax.map(one_block, numbers).reshape(count, -1)

def reference(hidden_in, norm_gain, w_query, w_keyval, w_out, doc_lengths):
    group = H // KVH
    width = H * HD // N_TP

    def replica(pair):
        stream, lengths = pair
        floats = stream.astype(jnp.float32)
        power = lax.optimization_barrier(jnp.mean(floats * floats, axis=-1, keepdims=True))
        normed = (floats * lax.rsqrt(power + eps_norm) * norm_gain[None, :]).astype(jnp.bfloat16)
        query = jnp.dot(normed, w_query, preferred_element_type=jnp.float32).reshape(SEQ, H, HD)
        keyval = jnp.dot(normed, w_keyval, preferred_element_type=jnp.float32)
        keys = keyval[:, :KVH * HD].reshape(SEQ, KVH, HD)
        values = keyval[:, KVH * HD:].reshape(SEQ, KVH, HD).astype(jnp.bfloat16)
        places, segment, positions = doc_layout(lengths, SEQ)
        query_rot = rotary(query, positions).astype(jnp.bfloat16)
        key_rot = rotary(keys, positions).astype(jnp.bfloat16)
        pieces = []
        for head_group in range(KVH):
            pieces.append(attend(query_rot[:, head_group * group:(head_group + 1) * group], key_rot[:, head_group], values[:, head_group], places, segment))
        context = jnp.concatenate(pieces, axis=1)

        def add_group(total, index):
            columns = lax.dynamic_slice_in_dim(context, index * width, width, 1)
            rows = lax.dynamic_slice_in_dim(w_out, index * width, width, 0)
            term = jnp.dot(columns, rows, preferred_element_type=jnp.float32)
            term = lax.optimization_barrier(term.astype(jnp.bfloat16)).astype(jnp.float32)
            return (total + term, None)
        summed, unused = lax.scan(add_group, jnp.zeros((SEQ, D), jnp.float32), jnp.arange(N_TP, dtype=jnp.int32))
        return (floats + summed).astype(jnp.bfloat16)
    outputs = lax.map(replica, (hidden_in.reshape(REPS, SEQ, D), doc_lengths))
    return outputs.reshape(TOKENS, D)
```

```python
import jax
import jax.numpy as jnp
from jax import lax
from jax.experimental import pallas as pl
from jax.experimental.pallas import tpu as pltpu
from jax.sharding import Mesh
from jax.sharding import PartitionSpec as P

H = 64
KVH = 8
HD = 128

theta_base = 1000000.0
eps_norm = 1e-06

TP = ("zl", "y", "c")
LOG2E = 1.4426950408889634


def shift(value, axis, by):
    size = lax.axis_size(axis)
    return lax.ppermute(value, axis, [(i, (i + by) % size) for i in range(size)])


def doc_starts(lengths, count):
    places = jnp.arange(count, dtype=jnp.int32)
    ends = jnp.cumsum(lengths)
    after = places[:, None] >= ends[None, :]
    return jnp.sum(jnp.where(after, lengths[None, :], 0), axis=1)


def gather_rep(own):
    half = own.shape[0] // 2
    got = {(0, 0): (own,), (0, 1): (shift(own, "zh", 1),)}
    for dz in (0, 1):
        mine = got[0, dz][0]
        ahead, behind = shift(mine, "x", 1), shift(mine, "x", -1)
        got[1, dz], got[3, dz] = (ahead,), (behind,)
        got[2, dz] = (shift(ahead[:half], "x", 1), shift(behind[half:], "x", -1))
    return got


def attention_kernel(start_ref, query_ref, key_ref, value_ref, cos_ref, sin_ref, out_ref, *, block, span):
    count = query_ref.shape[0]
    scale = HD ** (-0.5) * LOG2E
    for number in range(count // block):
        begin = number * block
        low = max(0, begin + block - span)
        rows = query_ref[begin : begin + block, :]
        turned = rows * cos_ref[begin : begin + block, :] + pltpu.roll(rows, HD // 2, 1) * sin_ref[begin : begin + block, :]
        scores = lax.dot_general(
            turned.astype(jnp.bfloat16),
            key_ref[low : begin + block, :],
            (((1,), (1,)), ((), ())),
            preferred_element_type=jnp.float32,
        )
        width = begin + block - low
        row_at = begin + lax.broadcasted_iota(jnp.int32, (block, width), 0)
        key_at = low + lax.broadcasted_iota(jnp.int32, (block, width), 1)
        allowed = (key_at >= start_ref[begin : begin + block, :]) & (key_at <= row_at)
        scores = jnp.where(allowed, scores, -1e30)
        top = jnp.max(scores, axis=-1, keepdims=True)
        weights = jnp.exp2((scores - top) * scale)
        probs = (weights / jnp.sum(weights, axis=-1, keepdims=True)).astype(jnp.bfloat16)
        blended = jnp.dot(probs, value_ref[low : begin + block, :], preferred_element_type=jnp.float32)
        out_ref[begin : begin + block, :] = blended.astype(jnp.bfloat16)


def attend(query, key, value, starts, cosine, sine):
    count, width = query.shape
    body = lambda *refs: attention_kernel(*refs, block=256, span=768)
    whole = pl.BlockSpec((count, HD), lambda h: (0, 0))
    head = pl.BlockSpec((count, HD), lambda h: (0, h))
    return pl.pallas_call(
        body,
        grid=(width // HD,),
        in_specs=[pl.BlockSpec((count, 1), lambda h: (0, 0)), head, whole, whole, whole, whole],
        out_specs=head,
        out_shape=jax.ShapeDtypeStruct((count, width), jnp.bfloat16),
        compiler_params=pltpu.CompilerParams(vmem_limit_bytes=32 * 1024 * 1024),
    )(starts[:, None], query, key, value, cosine, sine)


def shards(hidden_in, norm_gain, w_query, w_keyval, w_out, doc_lengths):
    tp_count = lax.axis_size(TP)
    token_count, width = hidden_in.shape
    core, at_y, at_zl = lax.axis_index("c"), lax.axis_index("y"), lax.axis_index("zl")
    at_x, at_zh = lax.axis_index("x"), lax.axis_index("zh")
    rows_here = w_query.shape[0]
    query_width = w_query.shape[1] // tp_count

    query_part = w_query.reshape(rows_here, tp_count, query_width)
    keyval_part = w_keyval.reshape(rows_here, 2, KVH, HD).transpose(0, 2, 1, 3).reshape(rows_here, tp_count, HD)
    packed = jnp.concatenate([query_part, keyval_part], axis=2).reshape(rows_here, -1)
    sliced = lax.all_to_all(packed, TP, split_axis=1, concat_axis=0, tiled=True)

    columns_here = w_out.shape[1]
    turned = w_out.T.reshape(columns_here, 2, 4, -1)
    by_y = lax.all_to_all(turned, "y", split_axis=2, concat_axis=0, tiled=True)
    by_y = by_y.reshape(4, columns_here, -1)
    keep = lax.dynamic_slice_in_dim(by_y, core * 2, 2, 0)
    give = lax.dynamic_slice_in_dim(by_y, (1 - core) * 2, 2, 0)
    come = shift(give, "c", 1)
    out_own = jnp.where(core == 0, jnp.stack([keep, come], 1), jnp.stack([come, keep], 1))
    out_own = out_own.reshape(4 * columns_here, -1)

    floats = hidden_in.astype(jnp.float32)
    power = jnp.mean(floats * floats, axis=-1, keepdims=True)
    normed = (floats * lax.rsqrt(power + eps_norm) * norm_gain[None, :]).astype(jnp.bfloat16)

    got = gather_rep(sliced)
    chunk = sliced.shape[0]
    projected = None
    for (dx, dz), pieces in got.items():
        rep_from = ((at_x - dx) % 4) * 2 + (at_zh - dz) % 2
        begin = rep_from * chunk
        for piece in pieces:
            part = lax.dynamic_slice_in_dim(normed, begin, piece.shape[0], 1)
            term = jnp.dot(part, piece, preferred_element_type=jnp.float32)
            projected = term if projected is None else projected + term
            begin = begin + piece.shape[0]

    starts = doc_starts(doc_lengths[0], token_count)
    positions = jnp.arange(token_count, dtype=jnp.int32) - starts
    half = HD // 2
    freqs = theta_base ** (-(jnp.arange(half, dtype=jnp.float32) * 2.0 / HD))
    angles = positions.astype(jnp.float32)[:, None] * freqs[None, :]
    cosine, sine = jnp.cos(angles), jnp.sin(angles)
    cosine = jnp.concatenate([cosine, cosine], axis=1)
    sine = jnp.concatenate([-sine, sine], axis=1)
    keyval = projected[:, query_width:]
    flipped = jnp.concatenate([keyval[:, half:], keyval[:, :half]], axis=1)
    own_keyval = jnp.where(core == 0, keyval * cosine + flipped * sine, keyval).astype(jnp.bfloat16)
    other_keyval = shift(own_keyval, "c", 1)
    key = jnp.where(core == 0, own_keyval, other_keyval)
    value = jnp.where(core == 0, other_keyval, own_keyval)
    context = attend(projected[:, :query_width], key, value, starts, cosine, sine)

    by_token = context.reshape(2, 4, 2, -1, query_width)
    mine = lax.dynamic_index_in_dim(by_token, core, 2, keepdims=False)
    theirs = lax.dynamic_index_in_dim(by_token, 1 - core, 2, keepdims=False)
    from_core = shift(theirs, "c", 1)
    from_chip = shift(mine, "zl", 1)
    from_both = lax.ppermute(theirs, ("zl", "c"), [(i, 3 - i) for i in range(4)])
    here = jnp.where(core == 0, jnp.stack([mine, from_core], 3), jnp.stack([from_core, mine], 3))
    there = jnp.where(core == 0, jnp.stack([from_chip, from_both], 3), jnp.stack([from_both, from_chip], 3))
    gathered = jnp.where(at_zl == 0, jnp.stack([here, there], 3), jnp.stack([there, here], 3))
    gathered = gathered.reshape(token_count // 2, -1)

    got = gather_rep(out_own)
    slices = [jnp.concatenate(got[d], 0) if len(got[d]) > 1 else got[d][0] for d in sorted(got)]
    mine_all = jnp.stack(slices, 0)
    other_all = shift(mine_all, "c", 1)
    both = jnp.where(core == 0, jnp.stack([mine_all, other_all], 1), jnp.stack([other_all, mine_all], 1))
    both = both.reshape(-1, both.shape[-1])
    partial = lax.dot_general(gathered, both, (((1,), (1,)), ((), ())), preferred_element_type=jnp.float32)
    partial = partial.astype(jnp.bfloat16).reshape(2, 4, -1, partial.shape[1])

    def for_y(by):
        return lax.dynamic_index_in_dim(partial, (at_y + by) % 4, 1, keepdims=False)

    summed = for_y(0).astype(jnp.float32)
    for by in (2, 1, -1):
        summed = summed + shift(for_y(by), "y", by).astype(jnp.float32)
    keep = lax.dynamic_index_in_dim(summed, at_zl, 0, keepdims=False).astype(jnp.bfloat16)
    give = lax.dynamic_index_in_dim(summed, 1 - at_zl, 0, keepdims=False).astype(jnp.bfloat16)
    come = shift(give, "zl", 1)
    share = keep.shape[0]
    pair = jnp.where(at_zl == 0, jnp.stack([keep, come], 1), jnp.stack([come, keep], 1))
    pair = pair.reshape(share, 2, 4, 2, -1)
    pair = jnp.take(pair, (at_x - jnp.arange(4)) % 4, axis=2)
    pair = jnp.take(pair, (at_zh - jnp.arange(2)) % 2, axis=3)
    total = pair.transpose(0, 2, 3, 1, 4).reshape(share, -1)
    own_rows = lax.dynamic_slice_in_dim(hidden_in, lax.axis_index(TP) * share, share, 0).astype(jnp.float32)
    return (own_rows + total.astype(jnp.float32)).astype(jnp.bfloat16)


def solution(mesh):
    fine = Mesh(mesh.devices.reshape(4, 2, 2, 4, 2), ("x", "zh", "zl", "y", "c"))
    rep, every = ("x", "zh"), ("x", "zh", "zl", "y", "c")
    in_specs = (P(rep, None), P(), P(every, None), P(every, None), P(None, every), P(rep, None))
    return jax.shard_map(shards, mesh=fine, in_specs=in_specs, out_specs=P(every, None), check_vma=False)
```

```python
import jax
import jax.numpy as jnp
from jax import lax
from jax.experimental import pallas as pl
from jax.experimental.pallas import tpu as pltpu
from jax.sharding import Mesh
from jax.sharding import PartitionSpec as P

H = 64
KVH = 8
HD = 128

theta_base = 1000000.0
eps_norm = 1e-06

TP = ("zl", "y", "c")
LOG2E = 1.4426950408889634
VMEM = 48 * 1024 * 1024


def shift(value, axis, by):
    size = lax.axis_size(axis)
    return lax.ppermute(value, axis, [(i, (i + by) % size) for i in range(size)])


def after(value, *earlier):
    return lax.optimization_barrier((value, *earlier))[0]


def doc_starts(lengths, count):
    places = jnp.arange(count, dtype=jnp.int32)
    ends = jnp.cumsum(lengths)
    after_end = places[:, None] >= ends[None, :]
    return jnp.sum(jnp.where(after_end, lengths[None, :], 0), axis=1)


def project(total, normed, pieces):
    count, block = normed.shape[0], 256
    width = pieces[0][0].shape[1]
    number = len(pieces)
    steps = jnp.stack([at // weight.shape[0] for weight, at in pieces]).astype(jnp.int32)

    def kernel(steps_ref, *refs):
        out_ref = refs[-1]
        value = None if total is None else refs[2 * number][...]
        for i in range(number):
            term = jnp.dot(refs[i][...], refs[number + i][...], preferred_element_type=jnp.float32)
            value = term if value is None else value + term
        out_ref[...] = value

    def rows_spec(i, depth):
        return pl.BlockSpec((block, depth), lambda m, steps_ref: (m, steps_ref[i]))

    in_specs = [rows_spec(i, weight.shape[0]) for i, (weight, _) in enumerate(pieces)]
    in_specs += [pl.BlockSpec(weight.shape, lambda m, steps_ref: (0, 0)) for weight, _ in pieces]
    args = [normed] * number + [weight for weight, _ in pieces]
    out_spec = pl.BlockSpec((block, width), lambda m, steps_ref: (m, 0))
    aliases = {}
    if total is not None:
        in_specs.append(out_spec)
        args.append(total)
        aliases = {2 * number + 1: 0}
    depth = sum(weight.shape[0] for weight, _ in pieces)
    return pl.pallas_call(
        kernel,
        grid_spec=pltpu.PrefetchScalarGridSpec(
            num_scalar_prefetch=1, grid=(count // block,), in_specs=in_specs, out_specs=out_spec
        ),
        out_shape=jax.ShapeDtypeStruct((count, width), jnp.float32),
        input_output_aliases=aliases,
        compiler_params=pltpu.CompilerParams(vmem_limit_bytes=VMEM),
        cost_estimate=pl.CostEstimate(
            flops=2 * count * depth * width, bytes_accessed=2 * depth * (count + width), transcendentals=0
        ),
    )(steps, *args)


def attention_kernel(start_ref, query_ref, key_ref, value_ref, cos_ref, sin_ref, out_ref, *, block, span):
    count = query_ref.shape[0]
    scale = HD ** (-0.5) * LOG2E
    for number in range(count // block):
        begin = number * block
        low = max(0, begin + block - span)
        rows = query_ref[begin : begin + block, :]
        turned = rows * cos_ref[begin : begin + block, :] + pltpu.roll(rows, HD // 2, 1) * sin_ref[begin : begin + block, :]
        scores = lax.dot_general(
            turned.astype(jnp.bfloat16),
            key_ref[low : begin + block, :],
            (((1,), (1,)), ((), ())),
            preferred_element_type=jnp.float32,
        )
        width = begin + block - low
        row_at = begin + lax.broadcasted_iota(jnp.int32, (block, width), 0)
        key_at = low + lax.broadcasted_iota(jnp.int32, (block, width), 1)
        allowed = (key_at >= start_ref[begin : begin + block, :]) & (key_at <= row_at)
        scores = jnp.where(allowed, scores, -1e30)
        top = jnp.max(scores, axis=-1, keepdims=True)
        weights = jnp.exp2((scores - top) * scale)
        probs = (weights / jnp.sum(weights, axis=-1, keepdims=True)).astype(jnp.bfloat16)
        blended = jnp.dot(probs, value_ref[low : begin + block, :], preferred_element_type=jnp.float32)
        out_ref[begin : begin + block, :] = blended.astype(jnp.bfloat16)


def attend(projected, heads, key, value, starts, cosine, sine):
    count = projected.shape[0]
    body = lambda *refs: attention_kernel(*refs, block=256, span=768)
    whole = pl.BlockSpec((count, HD), lambda h: (0, 0))
    head = pl.BlockSpec((count, HD), lambda h: (0, h))
    return pl.pallas_call(
        body,
        grid=(heads,),
        in_specs=[pl.BlockSpec((count, 1), lambda h: (0, 0)), head, whole, whole, whole, whole],
        out_specs=head,
        out_shape=jax.ShapeDtypeStruct((count, heads * HD), jnp.bfloat16),
        compiler_params=pltpu.CompilerParams(vmem_limit_bytes=VMEM),
        cost_estimate=pl.CostEstimate(
            flops=4 * heads * count * 640 * HD, bytes_accessed=8 * count * HD * heads, transcendentals=heads * count * 640
        ),
    )(starts[:, None], projected, key, value, cosine, sine)


def out_project(place, streams, weights):
    count = streams[0][0].shape[0]
    pairs = streams[0][0].shape[1]
    depth = weights[0][0].shape[1]
    slice_rows = 256
    columns = 4 * slice_rows
    per_owner = count // 8
    flat = [piece for stream in streams for piece in stream]

    def kernel(place_ref, *refs):
        context_refs, weight_refs = refs[: len(flat)], refs[len(flat) : len(flat) + len(weights)]
        out_refs, held = refs[len(flat) + len(weights) : -1], refs[-1]
        at_x, at_y, at_pair = place_ref[0], place_ref[1], place_ref[2]
        for number in range(len(flat)):
            stream, other = number // 4, number % 4
            group = jnp.bitwise_xor(at_pair, other)
            lane = pl.multiple_of(group * (len(streams) * pairs) + stream * pairs, pairs)
            for by in range(4):
                chip = lax.rem(at_y + by, 4)
                for zl in range(2):
                    row = pl.multiple_of(zl * 4 * per_owner + chip * per_owner, per_owner)
                    to = (by * 2 + zl) * per_owner
                    held[to : to + per_owner, pl.ds(lane, pairs)] = context_refs[number][pl.ds(row, per_owner), :]
        for number, (piece, back, row) in enumerate(weights):
            wide = piece.shape[0]
            lane = pl.multiple_of(lax.rem(at_x + 4 - back, 4) * slice_rows + row, 128)
            for by in range(4):
                term = lax.dot_general(
                    held[by * 2 * per_owner : (by + 1) * 2 * per_owner, :],
                    weight_refs[number][...],
                    (((1,), (1,)), ((), ())),
                    preferred_element_type=jnp.float32,
                )
                out_refs[by][:, pl.ds(lane, wide)] = term.astype(jnp.bfloat16)

    vmem = pl.BlockSpec(memory_space=pltpu.VMEM)
    return pl.pallas_call(
        kernel,
        in_specs=[pl.BlockSpec(memory_space=pltpu.SMEM)] + [vmem] * (len(flat) + len(weights)),
        out_specs=[vmem] * 4,
        out_shape=[jax.ShapeDtypeStruct((2 * per_owner, columns), jnp.bfloat16)] * 4,
        scratch_shapes=[pltpu.VMEM((count, depth), jnp.bfloat16)],
        compiler_params=pltpu.CompilerParams(vmem_limit_bytes=VMEM),
        cost_estimate=pl.CostEstimate(
            flops=2 * count * depth * columns, bytes_accessed=2 * depth * (count + columns), transcendentals=0
        ),
    )(place, *flat, *(piece for piece, _, _ in weights))


def finish(place, chunks, rows):
    share, width = rows.shape
    flat = [piece for chunk in chunks for piece in chunk]

    def kernel(place_ref, *refs):
        rows_ref, out_ref = refs[len(flat)], refs[-1]
        at_zh, at_pair = place_ref[3], place_ref[2]
        for x in range(4):
            for group in range(4):
                other = jnp.bitwise_xor(at_pair, group)
                found = []
                for dz in range(2):
                    parts = [refs[dz * 4 + i][:, x * 256 : (x + 1) * 256].astype(jnp.float32) for i in range(4)]
                    low = jnp.where(other % 2 == 0, parts[0], parts[1])
                    high = jnp.where(other % 2 == 0, parts[2], parts[3])
                    found.append(jnp.where(other < 2, low, high))
                for zh in range(2):
                    at = (x * 2 + zh) * 1024 + group * 256
                    total = jnp.where(at_zh == zh, found[0], found[1])
                    out_ref[:, at : at + 256] = (rows_ref[:, at : at + 256].astype(jnp.float32) + total).astype(jnp.bfloat16)

    vmem = pl.BlockSpec(memory_space=pltpu.VMEM)
    return pl.pallas_call(
        kernel,
        in_specs=[pl.BlockSpec(memory_space=pltpu.SMEM)] + [vmem] * (len(flat) + 1),
        out_specs=vmem,
        out_shape=jax.ShapeDtypeStruct((share, width), jnp.bfloat16),
        compiler_params=pltpu.CompilerParams(vmem_limit_bytes=VMEM),
    )(place, *flat, rows)


def swap_both(value):
    return lax.ppermute(value, ("zl", "c"), [(i, 3 - i) for i in range(4)])


def halves(ahead, behind):
    half = ahead.shape[0] // 2
    return shift(ahead[:half], "x", 1), shift(behind[half:], "x", -1)


def shards(hidden_in, norm_gain, w_query, w_keyval, w_out, doc_lengths):
    tp_count = lax.axis_size(TP)
    token_count, width = hidden_in.shape
    core, at_y, at_zl = lax.axis_index("c"), lax.axis_index("y"), lax.axis_index("zl")
    at_x, at_zh = lax.axis_index("x"), lax.axis_index("zh")
    place = jnp.stack([at_x, at_y, at_zl * 2 + core, at_zh]).astype(jnp.int32)
    rows_here = w_query.shape[0]
    chunk = rows_here * tp_count
    query_width = w_query.shape[1] // tp_count
    wide = query_width // 2

    query_part = w_query.reshape(rows_here, tp_count, query_width)
    keyval_part = w_keyval.reshape(rows_here, 2, KVH, HD).transpose(0, 2, 1, 3).reshape(rows_here, tp_count, HD)
    first = jnp.concatenate([query_part[:, :, :wide], keyval_part], axis=2).reshape(rows_here, -1)
    second = query_part[:, :, wide:].reshape(rows_here, -1)
    first = lax.all_to_all(first, TP, split_axis=1, concat_axis=0, tiled=True)
    second = lax.all_to_all(after(second, first), TP, split_axis=1, concat_axis=0, tiled=True)

    columns_here = w_out.shape[1]
    turned = w_out.T
    turned = jnp.stack([turned, shift(turned, "zh", 1)]).reshape(2, columns_here, 2, 4, -1)
    by_y = lax.all_to_all(after(turned, second), "y", split_axis=3, concat_axis=0, tiled=True)
    by_y = by_y.reshape(4, 2, columns_here, -1)
    keep = lax.dynamic_slice_in_dim(by_y, core * 2, 2, 0)
    give = lax.dynamic_slice_in_dim(by_y, (1 - core) * 2, 2, 0)
    come = shift(give, "c", 1)
    out_own = jnp.where(core == 0, jnp.stack([keep, come], 2), jnp.stack([come, keep], 2))

    floats = hidden_in.astype(jnp.float32)
    power = jnp.mean(floats * floats, axis=-1, keepdims=True)
    normed = (floats * lax.rsqrt(power + eps_norm) * norm_gain[None, :]).astype(jnp.bfloat16)
    normed = lax.optimization_barrier(normed)

    def at(dx, dz):
        return (((at_x - dx) % 4) * 2 + (at_zh - dz) % 2) * chunk

    half = chunk // 2
    a0 = first
    a1 = shift(a0, "zh", 1)
    a0_ahead, a0_behind = shift(a0, "x", 1), shift(a0, "x", -1)
    a0_far = halves(a0_ahead, a0_behind)
    b0 = after(second, a0_ahead, a0_behind)
    b0_ahead, b0_behind = shift(b0, "x", 1), shift(b0, "x", -1)
    b1 = shift(after(second, a1), "zh", 1)
    a1_ahead, a1_behind = shift(a1, "x", 1), shift(a1, "x", -1)
    b1_ahead, b1_behind = shift(b0_ahead, "zh", 1), shift(b0_behind, "zh", 1)
    a1_far = halves(a1_ahead, a1_behind)
    b0_far = halves(b0_ahead, b0_behind)
    b1_far = (shift(b0_far[0], "zh", 1), shift(b0_far[1], "zh", 1))

    def far(pieces, dz):
        return [(pieces[0], at(2, dz)), (pieces[1], at(2, dz) + half)]

    front = project(None, normed, [(a0, at(0, 0)), (a0_ahead, at(1, 0)), (a0_behind, at(3, 0)), (a1, at(0, 1))])
    front = project(front, normed, far(a0_far, 0))
    front = project(front, normed, [(a1_ahead, at(1, 1)), (a1_behind, at(3, 1))])
    front = project(front, normed, far(a1_far, 1))

    starts = doc_starts(doc_lengths[0], token_count)
    positions = jnp.arange(token_count, dtype=jnp.int32) - starts
    freqs = theta_base ** (-(jnp.arange(HD // 2, dtype=jnp.float32) * 2.0 / HD))
    angles = positions.astype(jnp.float32)[:, None] * freqs[None, :]
    cosine, sine = jnp.cos(angles), jnp.sin(angles)
    cosine = jnp.concatenate([cosine, cosine], axis=1)
    sine = jnp.concatenate([-sine, sine], axis=1)
    keyval = front[:, wide:]
    flipped = jnp.concatenate([keyval[:, HD // 2 :], keyval[:, : HD // 2]], axis=1)
    own_keyval = jnp.where(core == 0, keyval * cosine + flipped * sine, keyval).astype(jnp.bfloat16)
    other_keyval = shift(own_keyval, "c", 1)
    key = jnp.where(core == 0, own_keyval, other_keyval)
    value = jnp.where(core == 0, other_keyval, own_keyval)

    def spread(context):
        from_chip = shift(context, "zl", 1)
        return [context, shift(context, "c", 1), from_chip, shift(from_chip, "c", 1)]

    context_a = spread(attend(front, wide // HD, key, value, starts, cosine, sine))

    back = project(None, normed, [(b0, at(0, 0)), (b0_ahead, at(1, 0)), (b0_behind, at(3, 0)), (b1, at(0, 1))])
    back = project(back, normed, far(b0_far, 0) + [(b1_ahead, at(1, 1)), (b1_behind, at(3, 1))])
    back = project(back, normed, far(b1_far, 1))
    context_b = spread(attend(back, wide // HD, key, value, starts, cosine, sine))

    slices, chunks = [], []
    ready = (*a1_far, *b0_far)
    for dz in range(2):
        own = after(out_own[:, dz].reshape(4 * columns_here, -1), *ready)
        ahead, behind = shift(own, "x", 1), shift(own, "x", -1)
        away = halves(ahead, behind)
        slices.append([(own, 0, 0), (ahead, 1, 0), (behind, 3, 0), (away[0], 2, 0), (away[1], 2, 2 * columns_here)])
        ready = away
    for dz in range(2):
        parts = out_project(place, [context_a, context_b], slices[dz])
        total = parts[0].astype(jnp.float32)
        for by in (2, 1, 3):
            total = total + shift(parts[by], "y", by).astype(jnp.float32)
        total = total.reshape(4, -1, total.shape[1])
        pair = at_zl * 2 + core
        mine = lax.dynamic_index_in_dim(total, pair, 0, keepdims=False)
        theirs = [lax.dynamic_index_in_dim(total, pair ^ i, 0, keepdims=False).astype(jnp.bfloat16) for i in (1, 2, 3)]
        chunks.append([mine, shift(theirs[0], "c", 1), shift(theirs[1], "zl", 1), swap_both(theirs[2])])

    share = token_count // tp_count
    own_rows = lax.dynamic_slice_in_dim(hidden_in, lax.axis_index(TP) * share, share, 0)
    return finish(place, chunks, own_rows)


def solution(mesh):
    fine = Mesh(mesh.devices.reshape(4, 2, 2, 4, 2), ("x", "zh", "zl", "y", "c"))
    rep, every = ("x", "zh"), ("x", "zh", "zl", "y", "c")
    in_specs = (P(rep, None), P(), P(every, None), P(every, None), P(None, every), P(rep, None))
    return jax.shard_map(shards, mesh=fine, in_specs=in_specs, out_specs=P(every, None), check_vma=False)
```

```python
import jax
import jax.numpy as jnp
from jax import lax
from jax.experimental import pallas as pl
from jax.experimental.pallas import tpu as pltpu
from jax.sharding import Mesh
from jax.sharding import PartitionSpec as P

H = 64
KVH = 8
HD = 128

theta_base = 1000000.0
eps_norm = 1e-06

TP = ("zl", "y", "c")
LOG2E = 1.4426950408889634
VMEM = 48 * 1024 * 1024


def shift(value, axis, by):
    size = lax.axis_size(axis)
    return lax.ppermute(value, axis, [(i, (i + by) % size) for i in range(size)])


def after(value, *earlier):
    return lax.optimization_barrier((value, *earlier))[0]


def doc_starts(lengths, count):
    places = jnp.arange(count, dtype=jnp.int32)
    ends = jnp.cumsum(lengths)
    after_end = places[:, None] >= ends[None, :]
    return jnp.sum(jnp.where(after_end, lengths[None, :], 0), axis=1)


def project(total, normed, pieces):
    count, block = normed.shape[0], 256
    width = pieces[0][0].shape[1]
    number = len(pieces)
    steps = jnp.stack([at // weight.shape[0] for weight, at in pieces]).astype(jnp.int32)

    def kernel(steps_ref, *refs):
        out_ref = refs[-1]
        value = None if total is None else refs[2 * number][...]
        for i in range(number):
            term = jnp.dot(refs[i][...], refs[number + i][...], preferred_element_type=jnp.float32)
            value = term if value is None else value + term
        out_ref[...] = value

    def rows_spec(i, depth):
        return pl.BlockSpec((block, depth), lambda m, steps_ref: (m, steps_ref[i]))

    in_specs = [rows_spec(i, weight.shape[0]) for i, (weight, _) in enumerate(pieces)]
    in_specs += [pl.BlockSpec(weight.shape, lambda m, steps_ref: (0, 0)) for weight, _ in pieces]
    args = [normed] * number + [weight for weight, _ in pieces]
    out_spec = pl.BlockSpec((block, width), lambda m, steps_ref: (m, 0))
    aliases = {}
    if total is not None:
        in_specs.append(out_spec)
        args.append(total)
        aliases = {2 * number + 1: 0}
    depth = sum(weight.shape[0] for weight, _ in pieces)
    return pl.pallas_call(
        kernel,
        grid_spec=pltpu.PrefetchScalarGridSpec(
            num_scalar_prefetch=1, grid=(count // block,), in_specs=in_specs, out_specs=out_spec
        ),
        out_shape=jax.ShapeDtypeStruct((count, width), jnp.float32),
        input_output_aliases=aliases,
        compiler_params=pltpu.CompilerParams(vmem_limit_bytes=VMEM),
        cost_estimate=pl.CostEstimate(
            flops=2 * count * depth * width, bytes_accessed=2 * depth * (count + width), transcendentals=0
        ),
    )(steps, *args)


def attention_kernel(start_ref, query_ref, key_ref, value_ref, cos_ref, sin_ref, out_ref, *, block, span):
    count = query_ref.shape[0]
    scale = HD ** (-0.5) * LOG2E
    for number in range(count // block):
        begin = number * block
        low = max(0, begin + block - span)
        rows = query_ref[begin : begin + block, :]
        turned = rows * cos_ref[begin : begin + block, :] + pltpu.roll(rows, HD // 2, 1) * sin_ref[begin : begin + block, :]
        scores = lax.dot_general(
            turned.astype(jnp.bfloat16),
            key_ref[low : begin + block, :],
            (((1,), (1,)), ((), ())),
            preferred_element_type=jnp.float32,
        )
        width = begin + block - low
        row_at = begin + lax.broadcasted_iota(jnp.int32, (block, width), 0)
        key_at = low + lax.broadcasted_iota(jnp.int32, (block, width), 1)
        allowed = (key_at >= start_ref[begin : begin + block, :]) & (key_at <= row_at)
        scores = jnp.where(allowed, scores, -1e30)
        top = jnp.max(scores, axis=-1, keepdims=True)
        weights = jnp.exp2((scores - top) * scale)
        probs = (weights / jnp.sum(weights, axis=-1, keepdims=True)).astype(jnp.bfloat16)
        blended = jnp.dot(probs, value_ref[low : begin + block, :], preferred_element_type=jnp.float32)
        out_ref[begin : begin + block, :] = blended.astype(jnp.bfloat16)


def attend(projected, first, heads, key, value, starts, cosine, sine):
    count = projected.shape[0]
    body = lambda *refs: attention_kernel(*refs, block=256, span=768)
    whole = pl.BlockSpec((count, HD), lambda h: (0, 0))
    return pl.pallas_call(
        body,
        grid=(heads,),
        in_specs=[
            pl.BlockSpec((count, 1), lambda h: (0, 0)),
            pl.BlockSpec((count, HD), lambda h: (0, first + h)),
            *[whole] * 4,
        ],
        out_specs=pl.BlockSpec((count, HD), lambda h: (0, h)),
        out_shape=jax.ShapeDtypeStruct((count, heads * HD), jnp.bfloat16),
        compiler_params=pltpu.CompilerParams(vmem_limit_bytes=VMEM),
        cost_estimate=pl.CostEstimate(
            flops=4 * heads * count * 640 * HD, bytes_accessed=8 * count * HD * heads, transcendentals=heads * count * 640
        ),
    )(starts[:, None], projected, key, value, cosine, sine)


def out_project(place, streams, weights):
    count = streams[0][0].shape[0]
    pairs = streams[0][0].shape[1]
    depth = weights[0][0].shape[1]
    slice_rows = 256
    columns = 4 * slice_rows
    per_owner = count // 8
    flat = [piece for stream in streams for piece in stream]

    def kernel(place_ref, *refs):
        context_refs, weight_refs = refs[: len(flat)], refs[len(flat) : len(flat) + len(weights)]
        out_refs, held = refs[len(flat) + len(weights) : -1], refs[-1]
        at_x, at_y, at_pair = place_ref[0], place_ref[1], place_ref[2]
        for number in range(len(flat)):
            stream, other = number // 4, number % 4
            group = jnp.bitwise_xor(at_pair, other)
            lane = pl.multiple_of(group * (len(streams) * pairs) + stream * pairs, pairs)
            for by in range(4):
                chip = lax.rem(at_y + by, 4)
                for zl in range(2):
                    row = pl.multiple_of(zl * 4 * per_owner + chip * per_owner, per_owner)
                    to = (by * 2 + zl) * per_owner
                    held[to : to + per_owner, pl.ds(lane, pairs)] = context_refs[number][pl.ds(row, per_owner), :]
        for number, (piece, back, row) in enumerate(weights):
            wide = piece.shape[0]
            lane = pl.multiple_of(lax.rem(at_x + 4 - back, 4) * slice_rows + row, 128)
            for by in range(4):
                term = lax.dot_general(
                    held[by * 2 * per_owner : (by + 1) * 2 * per_owner, :],
                    weight_refs[number][...],
                    (((1,), (1,)), ((), ())),
                    preferred_element_type=jnp.float32,
                )
                out_refs[by][:, pl.ds(lane, wide)] = term.astype(jnp.bfloat16)

    vmem = pl.BlockSpec(memory_space=pltpu.VMEM)
    return pl.pallas_call(
        kernel,
        in_specs=[pl.BlockSpec(memory_space=pltpu.SMEM)] + [vmem] * (len(flat) + len(weights)),
        out_specs=[vmem] * 4,
        out_shape=[jax.ShapeDtypeStruct((2 * per_owner, columns), jnp.bfloat16)] * 4,
        scratch_shapes=[pltpu.VMEM((count, depth), jnp.bfloat16)],
        compiler_params=pltpu.CompilerParams(vmem_limit_bytes=VMEM),
        cost_estimate=pl.CostEstimate(
            flops=2 * count * depth * columns, bytes_accessed=2 * depth * (count + columns), transcendentals=0
        ),
    )(place, *flat, *(piece for piece, _, _ in weights))


def finish(place, chunks, rows):
    share, width = rows.shape
    flat = [piece for chunk in chunks for piece in chunk]

    def kernel(place_ref, *refs):
        rows_ref, out_ref = refs[len(flat)], refs[-1]
        at_zh, at_pair = place_ref[3], place_ref[2]
        left = lax.broadcasted_iota(jnp.int32, (share, HD), 1) < HD // 2

        def part(dz, group, lanes):
            parts = [refs[dz * 4 + i][:, lanes].astype(jnp.float32) for i in range(4)]
            other = jnp.bitwise_xor(at_pair, group)
            low = jnp.where(other % 2 == 0, parts[0], parts[1])
            high = jnp.where(other % 2 == 0, parts[2], parts[3])
            return jnp.where(other < 2, low, high)

        for x in range(4):
            for zl in range(2):
                for pair in range(2):
                    lanes = slice(x * 256 + pair * HD, x * 256 + (pair + 1) * HD)
                    found = [[part(dz, zl * 2 + c, lanes) for c in range(2)] for dz in range(2)]
                    for zh in range(2):
                        zero, one = [jnp.where(at_zh == zh, found[0][c], found[1][c]) for c in range(2)]
                        both = (
                            jnp.where(left, zero, pltpu.roll(one, HD // 2, 1)),
                            jnp.where(left, pltpu.roll(zero, HD // 2, 1), one),
                        )
                        for i in range(2):
                            at = (x * 2 + zh) * 1024 + zl * 512 + (pair * 2 + i) * HD
                            here = rows_ref[:, at : at + HD].astype(jnp.float32)
                            out_ref[:, at : at + HD] = (here + both[i]).astype(jnp.bfloat16)

    vmem = pl.BlockSpec(memory_space=pltpu.VMEM)
    return pl.pallas_call(
        kernel,
        in_specs=[pl.BlockSpec(memory_space=pltpu.SMEM)] + [vmem] * (len(flat) + 1),
        out_specs=vmem,
        out_shape=jax.ShapeDtypeStruct((share, width), jnp.bfloat16),
        compiler_params=pltpu.CompilerParams(vmem_limit_bytes=VMEM),
    )(place, *flat, rows)


def pack_projection(w_query, w_keyval, tp_count):
    rows, wide = w_query.shape[0], w_query.shape[1] // tp_count

    def kernel(query_ref, keyval_ref, out_ref):
        for group in range(tp_count):
            to = slice(group * rows, (group + 1) * rows)
            out_ref[to, :wide] = query_ref[:, group * wide : (group + 1) * wide]
            at = (group % 2 * KVH + group // 2) * HD
            out_ref[to, wide:] = keyval_ref[:, at : at + HD]

    vmem = pl.BlockSpec(memory_space=pltpu.VMEM)
    return pl.pallas_call(
        kernel,
        in_specs=[vmem, vmem],
        out_specs=vmem,
        out_shape=jax.ShapeDtypeStruct((tp_count * rows, wide + HD), jnp.bfloat16),
        compiler_params=pltpu.CompilerParams(vmem_limit_bytes=VMEM),
    )(w_query, w_keyval)


def pack_output(turned):
    columns, rows = turned.shape[0], turned.shape[1] // 8

    def kernel(in_ref, out_ref):
        for y in range(4):
            for zl in range(2):
                at = (zl * 4 + y) * rows
                out_ref[y * columns : (y + 1) * columns, zl * rows : (zl + 1) * rows] = in_ref[:, at : at + rows]

    vmem = pl.BlockSpec(memory_space=pltpu.VMEM)
    return pl.pallas_call(
        kernel,
        in_specs=[vmem],
        out_specs=vmem,
        out_shape=jax.ShapeDtypeStruct((4 * columns, 2 * rows), jnp.bfloat16),
        compiler_params=pltpu.CompilerParams(vmem_limit_bytes=VMEM),
    )(turned)


def swap_both(value):
    return lax.ppermute(value, ("zl", "c"), [(i, 3 - i) for i in range(4)])


def halves(ahead, behind):
    half = ahead.shape[0] // 2
    return shift(ahead[:half], "x", 1), shift(behind[half:], "x", -1)


def shards(hidden_in, norm_gain, w_query, w_keyval, w_out, doc_lengths):
    tp_count = lax.axis_size(TP)
    token_count, width = hidden_in.shape
    core, at_y, at_zl = lax.axis_index("c"), lax.axis_index("y"), lax.axis_index("zl")
    at_x, at_zh = lax.axis_index("x"), lax.axis_index("zh")
    place = jnp.stack([at_x, at_y, at_zl * 2 + core, at_zh]).astype(jnp.int32)
    chunk = w_query.shape[0] * tp_count
    query_width = w_query.shape[1] // tp_count
    wide = query_width // 2
    half, quarter = chunk // 2, chunk // 4

    floats = hidden_in.astype(jnp.float32)
    power = jnp.mean(floats * floats, axis=-1, keepdims=True)
    normed = (floats * lax.rsqrt(power + eps_norm) * norm_gain[None, :]).astype(jnp.bfloat16)

    own = lax.all_to_all(pack_projection(w_query, w_keyval, tp_count), TP, split_axis=0, concat_axis=0, tiled=True)
    out_here = pack_output(w_out.T)
    out_zh = shift(out_here, "zh", 1)
    own, normed = lax.optimization_barrier((own, normed))

    def at(dx, dz):
        return (((at_x - dx) % 4) * 2 + (at_zh - dz) % 2) * chunk

    ahead, behind, other = shift(own, "x", 1), shift(own, "x", -1), shift(own, "zh", 1)
    ahead, behind, other = lax.optimization_barrier((ahead, behind, other))
    front = project(
        None, normed, [(own, at(0, 0)), (ahead, at(1, 0)), (behind, at(3, 0)), (other, at(0, 1))]
    )
    far_low, far_high = shift(ahead[:half], "x", 1), shift(behind[half:], "x", -1)
    other_ahead_low, other_behind_low = shift(other[:half], "x", 1), shift(other[:half], "x", -1)
    other_high = shift(jnp.concatenate([ahead[half:], behind[half:]]), "zh", 1)
    front, out_zh = lax.optimization_barrier((front, out_zh))

    out_both = jnp.concatenate([out_here.reshape(4, -1, out_here.shape[1]), out_zh.reshape(4, -1, out_here.shape[1])], 1)
    out_both = lax.all_to_all(out_both, "y", split_axis=0, concat_axis=0, tiled=True)

    far_low, far_high, other_ahead_low, other_behind_low, other_high = lax.optimization_barrier(
        (far_low, far_high, other_ahead_low, other_behind_low, other_high)
    )
    front = project(
        front,
        normed,
        [
            (far_low, at(2, 0)),
            (far_high, at(2, 0) + half),
            (other_ahead_low, at(1, 1)),
            (other_behind_low, at(3, 1)),
            (other_high[:half], at(1, 1) + half),
            (other_high[half:], at(3, 1) + half),
        ],
    )
    other_far = (
        shift(other_ahead_low[:quarter], "x", 1),
        shift(other_behind_low[quarter:], "x", -1),
        shift(far_high, "zh", 1),
    )
    front, *other_far = lax.optimization_barrier((front, *other_far))
    front = project(
        front,
        normed,
        [(other_far[0], at(2, 1)), (other_far[1], at(2, 1) + quarter), (other_far[2], at(2, 1) + half)],
    )

    starts = doc_starts(doc_lengths[0], token_count)
    positions = jnp.arange(token_count, dtype=jnp.int32) - starts
    freqs = theta_base ** (-(jnp.arange(HD // 2, dtype=jnp.float32) * 2.0 / HD))
    angles = positions.astype(jnp.float32)[:, None] * freqs[None, :]
    cosine, sine = jnp.cos(angles), jnp.sin(angles)
    cosine = jnp.concatenate([cosine, cosine], axis=1)
    sine = jnp.concatenate([-sine, sine], axis=1)
    keyval = front[:, query_width:]
    flipped = jnp.concatenate([keyval[:, HD // 2 :], keyval[:, : HD // 2]], axis=1)
    own_keyval = jnp.where(core == 0, keyval * cosine + flipped * sine, keyval).astype(jnp.bfloat16)
    other_keyval = shift(own_keyval, "c", 1)
    key = jnp.where(core == 0, own_keyval, other_keyval)
    value = jnp.where(core == 0, other_keyval, own_keyval)

    def spread(context):
        from_chip = shift(context, "zl", 1)
        return [context, shift(context, "c", 1), from_chip, shift(from_chip, "c", 1)]

    heads = wide // HD
    context_a = attend(front, 0, heads, key, value, starts, cosine, sine)
    context_b = attend(front, heads, heads, after(key, context_a), value, starts, cosine, sine)
    context_a, context_b = spread(context_a), spread(context_b)

    slices, chunks = [], []
    columns_here = w_out.shape[1]
    out_both = out_both.reshape(4, 2, columns_here, -1)
    ready = other_far[:2]
    for dz in range(2):
        own = after(out_both[:, dz].reshape(4 * columns_here, -1), *ready)
        ahead, behind = shift(own, "x", 1), shift(own, "x", -1)
        ready = (ahead, behind)
        away = halves(ahead, behind)
        slices.append([(own, 0, 0), (ahead, 1, 0), (behind, 3, 0), (away[0], 2, 0), (away[1], 2, 2 * columns_here)])
    for dz in range(2):
        parts = out_project(place, [context_a, context_b], slices[dz])
        total = parts[0].astype(jnp.float32)
        for by in (2, 1, 3):
            total = total + shift(parts[by], "y", by).astype(jnp.float32)
        total = total.reshape(4, -1, total.shape[1])
        pair = at_zl * 2 + core
        mine = lax.dynamic_index_in_dim(total, pair, 0, keepdims=False)
        theirs = [lax.dynamic_index_in_dim(total, pair ^ i, 0, keepdims=False).astype(jnp.bfloat16) for i in (1, 2, 3)]
        chunks.append([mine, shift(theirs[0], "c", 1), shift(theirs[1], "zl", 1), swap_both(theirs[2])])

    share = token_count // tp_count
    own_rows = lax.dynamic_slice_in_dim(hidden_in, lax.axis_index(TP) * share, share, 0)
    return finish(place, chunks, own_rows)


def solution(mesh):
    fine = Mesh(mesh.devices.reshape(4, 2, 2, 4, 2), ("x", "zh", "zl", "y", "c"))
    rep, every = ("x", "zh"), ("x", "zh", "zl", "y", "c")
    in_specs = (P(rep, None), P(), P(every, None), P(every, None), P(None, every), P(rep, None))
    return jax.shard_map(shards, mesh=fine, in_specs=in_specs, out_specs=P(every, None), check_vma=False)
```

```python
import jax
import jax.numpy as jnp
from jax import lax
from jax.experimental import pallas as pl
from jax.experimental.pallas import tpu as pltpu
from jax.sharding import Mesh
from jax.sharding import PartitionSpec as P

H = 64
KVH = 8
HD = 128

theta_base = 1000000.0
eps_norm = 1e-06

TP = ("zl", "y", "c")
LOG2E = 1.4426950408889634
VMEM = 48 * 1024 * 1024


def shift(value, axis, by):
    size = lax.axis_size(axis)
    return lax.ppermute(value, axis, [(i, (i + by) % size) for i in range(size)])


def after(value, *earlier):
    return lax.optimization_barrier((value, *earlier))[0]


def doc_starts(lengths, count):
    places = jnp.arange(count, dtype=jnp.int32)
    ends = jnp.cumsum(lengths)
    after_end = places[:, None] >= ends[None, :]
    return jnp.sum(jnp.where(after_end, lengths[None, :], 0), axis=1)


def normalize(hidden, gain):
    count, width = hidden.shape
    block = 128

    def kernel(hidden_ref, gain_ref, out_ref):
        floats = hidden_ref[...].astype(jnp.float32)
        power = jnp.mean(floats * floats, axis=-1, keepdims=True)
        out_ref[...] = (floats * lax.rsqrt(power + eps_norm) * gain_ref[...]).astype(jnp.bfloat16)

    rows = pl.BlockSpec((block, width), lambda m: (m, 0))
    return pl.pallas_call(
        kernel,
        grid=(count // block,),
        in_specs=[rows, pl.BlockSpec((1, width), lambda m: (0, 0))],
        out_specs=rows,
        out_shape=jax.ShapeDtypeStruct((count, width), jnp.bfloat16),
        compiler_params=pltpu.CompilerParams(vmem_limit_bytes=VMEM),
        cost_estimate=pl.CostEstimate(flops=6 * count * width, bytes_accessed=4 * count * width, transcendentals=count),
    )(hidden, gain[None, :])


def project(total, normed, pieces):
    count, block = normed.shape[0], 512
    width = pieces[0][0].shape[1]
    number = len(pieces)
    steps = jnp.stack([at // rows for _, _, rows, at in pieces]).astype(jnp.int32)

    def kernel(steps_ref, *refs):
        out_ref = refs[-1]
        value = None if total is None else refs[2 * number][...]
        for i in range(number):
            term = jnp.dot(refs[i][...], refs[number + i][...], preferred_element_type=jnp.float32)
            value = term if value is None else value + term
        out_ref[...] = value

    def rows_spec(i, rows):
        return pl.BlockSpec((block, rows), lambda m, steps_ref: (m, steps_ref[i]))

    def weight_spec(rows, at_block):
        return pl.BlockSpec((rows, width), lambda m, steps_ref: (at_block, 0))

    in_specs = [rows_spec(i, rows) for i, (_, _, rows, _) in enumerate(pieces)]
    in_specs += [weight_spec(rows, at_block) for _, at_block, rows, _ in pieces]
    args = [normed] * number + [weights for weights, _, _, _ in pieces]
    out_spec = pl.BlockSpec((block, width), lambda m, steps_ref: (m, 0))
    aliases = {}
    if total is not None:
        in_specs.append(out_spec)
        args.append(total)
        aliases = {2 * number + 1: 0}
    depth = sum(rows for _, _, rows, _ in pieces)
    return pl.pallas_call(
        kernel,
        grid_spec=pltpu.PrefetchScalarGridSpec(
            num_scalar_prefetch=1, grid=(count // block,), in_specs=in_specs, out_specs=out_spec
        ),
        out_shape=jax.ShapeDtypeStruct((count, width), jnp.float32),
        input_output_aliases=aliases,
        compiler_params=pltpu.CompilerParams(vmem_limit_bytes=VMEM),
        cost_estimate=pl.CostEstimate(
            flops=2 * count * depth * width, bytes_accessed=2 * depth * (count + width), transcendentals=0
        ),
    )(steps, *args)


def attention_kernel(
    lengths_ref, core_ref, query_ref, own_ref, other_ref, cos_ref, sin_ref, out_ref, key_ref, value_ref, *, block, span
):
    count = query_ref.shape[0]
    scale = HD ** (-0.5) * LOG2E

    @pl.when((pl.program_id(0) == 0) & (core_ref[0] == 0))
    def _():
        key_ref[...], value_ref[...] = own_ref[...], other_ref[...]

    @pl.when((pl.program_id(0) == 0) & (core_ref[0] != 0))
    def _():
        key_ref[...], value_ref[...] = other_ref[...], own_ref[...]

    for number in range(count // block):
        begin = number * block
        low = max(0, begin + block - span)
        rows = query_ref[begin : begin + block, :]
        turned = rows * cos_ref[begin : begin + block, :] + pltpu.roll(rows, HD // 2, 1) * sin_ref[begin : begin + block, :]
        scores = lax.dot_general(
            turned.astype(jnp.bfloat16),
            key_ref[low : begin + block, :],
            (((1,), (1,)), ((), ())),
            preferred_element_type=jnp.float32,
        )
        width = begin + block - low
        place = begin + lax.broadcasted_iota(jnp.int32, (block, 1), 0)
        start, end = jnp.zeros((block, 1), jnp.int32), 0
        for document in range(lengths_ref.shape[1]):
            end = end + lengths_ref[0, document]
            start = jnp.where(place >= end, end, start)
        key_at = low + lax.broadcasted_iota(jnp.int32, (block, width), 1)
        allowed = (key_at >= start) & (key_at <= place)
        scores = jnp.where(allowed, scores, -1e30)
        top = jnp.max(scores, axis=-1, keepdims=True)
        weights = jnp.exp2((scores - top) * scale)
        probs = (weights / jnp.sum(weights, axis=-1, keepdims=True)).astype(jnp.bfloat16)
        blended = jnp.dot(probs, value_ref[low : begin + block, :], preferred_element_type=jnp.float32)
        out_ref[begin : begin + block, :] = blended.astype(jnp.bfloat16)


def attend(projected, first, heads, keyval, other_keyval, lengths, core, cosine, sine):
    count = projected.shape[0]
    body = lambda *refs: attention_kernel(*refs, block=256, span=768)
    whole = pl.BlockSpec((count, HD), lambda h: (0, 0))
    smem = pl.BlockSpec(memory_space=pltpu.SMEM)
    return pl.pallas_call(
        body,
        grid=(heads,),
        in_specs=[smem, smem, pl.BlockSpec((count, HD), lambda h: (0, first + h)), *[whole] * 4],
        out_specs=pl.BlockSpec((count, HD), lambda h: (0, h)),
        out_shape=jax.ShapeDtypeStruct((count, heads * HD), jnp.bfloat16),
        scratch_shapes=[pltpu.VMEM((count, HD), jnp.bfloat16)] * 2,
        compiler_params=pltpu.CompilerParams(vmem_limit_bytes=VMEM),
        cost_estimate=pl.CostEstimate(
            flops=4 * heads * count * 640 * HD, bytes_accessed=8 * count * HD * heads, transcendentals=heads * count * 640
        ),
    )(lengths, core, projected, keyval, other_keyval, cosine, sine)


def out_project(place, contexts, arrays, weights):
    joined = len(contexts) == 1
    flat = contexts if joined else [piece for stream in contexts for piece in stream]
    count, depth = flat[0].shape[0], arrays[0].shape[1]
    each, columns = 256, 1024
    per_owner = count // 8

    def kernel(place_ref, *refs):
        context_refs, array_refs = refs[: len(flat)], refs[len(flat) : len(flat) + len(arrays)]
        out_refs = refs[len(flat) + len(arrays) :]
        at_x, at_y, at_pair = place_ref[0], place_ref[1], place_ref[2]
        held = context_refs[0] if joined else out_refs[4]
        if not joined:
            pairs = flat[0].shape[1]
            for number in range(len(flat)):
                stream, other = number // 4, number % 4
                group = jnp.bitwise_xor(at_pair, other)
                lane = pl.multiple_of(group * (len(contexts) * pairs) + stream * pairs, pairs)
                for by in range(4):
                    chip = lax.rem(at_y + by, 4)
                    for zl in range(2):
                        row = pl.multiple_of(zl * 4 * per_owner + chip * per_owner, per_owner)
                        to = (by * 2 + zl) * per_owner
                        held[to : to + per_owner, pl.ds(lane, pairs)] = context_refs[number][pl.ds(row, per_owner), :]
        for array, row, rows, dx, column in weights:
            lane = pl.multiple_of(lax.rem(at_x + 4 - dx, 4) * each + column, HD)
            for by in range(4):
                term = lax.dot_general(
                    held[by * 2 * per_owner : (by + 1) * 2 * per_owner, :],
                    array_refs[array][row : row + rows, :],
                    (((1,), (1,)), ((), ())),
                    preferred_element_type=jnp.float32,
                )
                out_refs[by][:, pl.ds(lane, rows)] = term.astype(jnp.bfloat16)

    vmem = pl.BlockSpec(memory_space=pltpu.VMEM)
    out_shape = [jax.ShapeDtypeStruct((2 * per_owner, columns), jnp.bfloat16)] * 4
    if not joined:
        out_shape.append(jax.ShapeDtypeStruct((count, depth), jnp.bfloat16))
    return pl.pallas_call(
        kernel,
        in_specs=[pl.BlockSpec(memory_space=pltpu.SMEM)] + [vmem] * (len(flat) + len(arrays)),
        out_specs=[vmem] * len(out_shape),
        out_shape=out_shape,
        compiler_params=pltpu.CompilerParams(vmem_limit_bytes=VMEM),
        cost_estimate=pl.CostEstimate(
            flops=2 * count * depth * columns, bytes_accessed=2 * depth * (count + columns), transcendentals=0
        ),
    )(place, *flat, *arrays)


def finish(place, chunks, rows):
    share, width = rows.shape
    flat = [piece for chunk in chunks for piece in chunk]

    def kernel(place_ref, *refs):
        rows_ref, out_ref = refs[len(flat)], refs[-1]
        at_zh, at_pair = place_ref[3], place_ref[2]
        left = lax.broadcasted_iota(jnp.int32, (share, HD), 1) < HD // 2

        def part(dz, group, lanes):
            parts = [refs[dz * 4 + i][:, lanes].astype(jnp.float32) for i in range(4)]
            other = jnp.bitwise_xor(at_pair, group)
            low = jnp.where(other % 2 == 0, parts[0], parts[1])
            high = jnp.where(other % 2 == 0, parts[2], parts[3])
            return jnp.where(other < 2, low, high)

        for x in range(4):
            for zl in range(2):
                for pair in range(2):
                    lanes = slice(x * 256 + pair * HD, x * 256 + (pair + 1) * HD)
                    found = [[part(dz, zl * 2 + c, lanes) for c in range(2)] for dz in range(2)]
                    for zh in range(2):
                        zero, one = [jnp.where(at_zh == zh, found[0][c], found[1][c]) for c in range(2)]
                        both = (
                            jnp.where(left, zero, pltpu.roll(one, HD // 2, 1)),
                            jnp.where(left, pltpu.roll(zero, HD // 2, 1), one),
                        )
                        for i in range(2):
                            at = (x * 2 + zh) * 1024 + zl * 512 + (pair * 2 + i) * HD
                            here = rows_ref[:, at : at + HD].astype(jnp.float32)
                            out_ref[:, at : at + HD] = (here + both[i]).astype(jnp.bfloat16)

    vmem = pl.BlockSpec(memory_space=pltpu.VMEM)
    return pl.pallas_call(
        kernel,
        in_specs=[pl.BlockSpec(memory_space=pltpu.SMEM)] + [vmem] * (len(flat) + 1),
        out_specs=vmem,
        out_shape=jax.ShapeDtypeStruct((share, width), jnp.bfloat16),
        compiler_params=pltpu.CompilerParams(vmem_limit_bytes=VMEM),
    )(place, *flat, rows)


def pack_projection(w_query, w_keyval, tp_count):
    rows, wide = w_query.shape[0], w_query.shape[1] // tp_count

    def kernel(query_ref, keyval_ref, out_ref):
        for group in range(tp_count):
            to = slice(group * rows, (group + 1) * rows)
            out_ref[to, :wide] = query_ref[:, group * wide : (group + 1) * wide]
            at = (group % 2 * KVH + group // 2) * HD
            out_ref[to, wide:] = keyval_ref[:, at : at + HD]

    vmem = pl.BlockSpec(memory_space=pltpu.VMEM)
    return pl.pallas_call(
        kernel,
        in_specs=[vmem, vmem],
        out_specs=vmem,
        out_shape=jax.ShapeDtypeStruct((tp_count * rows, wide + HD), jnp.bfloat16),
        compiler_params=pltpu.CompilerParams(vmem_limit_bytes=VMEM),
    )(w_query, w_keyval)


def pack_output(turned):
    columns, rows = turned.shape[0], turned.shape[1] // 8

    def kernel(in_ref, out_ref):
        for y in range(4):
            for zl in range(2):
                at = (zl * 4 + y) * rows
                out_ref[y * columns : (y + 1) * columns, zl * rows : (zl + 1) * rows] = in_ref[:, at : at + rows]

    vmem = pl.BlockSpec(memory_space=pltpu.VMEM)
    return pl.pallas_call(
        kernel,
        in_specs=[vmem],
        out_specs=vmem,
        out_shape=jax.ShapeDtypeStruct((4 * columns, 2 * rows), jnp.bfloat16),
        compiler_params=pltpu.CompilerParams(vmem_limit_bytes=VMEM),
    )(turned)


def pick(arrays, outputs):
    def kernel(*refs):
        for out_ref, parts in zip(refs[len(arrays) :], outputs):
            to = 0
            for array, row, rows in parts:
                out_ref[to : to + rows, :] = refs[array][row : row + rows, :]
                to += rows

    vmem = pl.BlockSpec(memory_space=pltpu.VMEM)
    width = arrays[0].shape[1]
    return pl.pallas_call(
        kernel,
        in_specs=[vmem] * len(arrays),
        out_specs=[vmem] * len(outputs),
        out_shape=[jax.ShapeDtypeStruct((sum(p[2] for p in parts), width), jnp.bfloat16) for parts in outputs],
        compiler_params=pltpu.CompilerParams(vmem_limit_bytes=VMEM),
    )(*arrays)


def swap_both(value):
    return lax.ppermute(value, ("zl", "c"), [(i, 3 - i) for i in range(4)])


def shards(hidden_in, norm_gain, w_query, w_keyval, w_out, doc_lengths):
    tp_count = lax.axis_size(TP)
    token_count, width = hidden_in.shape
    core, at_y, at_zl = lax.axis_index("c"), lax.axis_index("y"), lax.axis_index("zl")
    at_x, at_zh = lax.axis_index("x"), lax.axis_index("zh")
    place = jnp.stack([at_x, at_y, at_zl * 2 + core, at_zh]).astype(jnp.int32)
    chunk = w_query.shape[0] * tp_count
    query_width = w_query.shape[1] // tp_count
    wide = query_width // 2
    half, quarter = chunk // 2, chunk // 4

    own = lax.all_to_all(pack_projection(w_query, w_keyval, tp_count), TP, split_axis=0, concat_axis=0, tiled=True)
    normed = normalize(hidden_in, norm_gain)
    starts = doc_starts(doc_lengths[0], token_count)
    positions = jnp.arange(token_count, dtype=jnp.int32) - starts
    freqs = theta_base ** (-(jnp.arange(HD // 2, dtype=jnp.float32) * 2.0 / HD))
    angles = positions.astype(jnp.float32)[:, None] * freqs[None, :]
    cosine, sine = jnp.cos(angles), jnp.sin(angles)
    cosine = jnp.concatenate([cosine, cosine], axis=1)
    sine = jnp.concatenate([-sine, sine], axis=1)
    packed = pack_output(w_out.T)
    own, normed, cosine, sine, packed = lax.optimization_barrier((own, normed, cosine, sine, packed))

    def at(dx, dz):
        return (((at_x - dx) % 4) * 2 + (at_zh - dz) % 2) * chunk

    ahead, behind, other = shift(own, "x", 1), shift(own, "x", -1), shift(own, "zh", 1)

    out_rows = lax.all_to_all(packed, "y", split_axis=0, concat_axis=0, tiled=True)

    over, far_low, far_high = pick(
        [ahead, behind], [[(0, half, half), (1, half, half)], [(0, 0, half)], [(1, half, half)]]
    )
    over, far_low, far_high = shift(over, "zh", 1), shift(far_low, "x", 1), shift(far_high, "x", -1)
    (other_low,) = pick([other], [[(0, 0, half)]])
    low_ahead, low_behind = shift(other_low, "x", 1), shift(other_low, "x", -1)
    front = project(
        None,
        normed,
        [(own, 0, chunk, at(0, 0)), (ahead, 0, chunk, at(1, 0)), (behind, 0, chunk, at(3, 0)), (other, 0, chunk, at(0, 1))],
    )
    front, far_low, far_high, low_ahead, low_behind, over = lax.optimization_barrier(
        (front, far_low, far_high, low_ahead, low_behind, over)
    )
    up_far = shift(low_ahead[:quarter], "x", 1)
    down_far = shift(low_behind[quarter:], "x", -1)
    over_far = shift(far_high, "zh", 1)
    front = project(
        front,
        normed,
        [
            (far_low, 0, half, at(2, 0)),
            (far_high, 0, half, at(2, 0) + half),
            (low_ahead, 0, half, at(1, 1)),
            (low_behind, 0, half, at(3, 1)),
            (over, 0, half, at(1, 1) + half),
            (over, 1, half, at(3, 1) + half),
        ],
    )

    out_own, front = lax.optimization_barrier((out_rows, front))
    out_up, out_down = [shift(out_own, "x", 1)], [shift(out_own, "x", -1)]

    front, up_far, down_far, over_far = lax.optimization_barrier((front, up_far, down_far, over_far))
    front = project(
        front,
        normed,
        [
            (up_far, 0, quarter, at(2, 1)),
            (down_far, 0, quarter, at(2, 1) + quarter),
            (over_far, 0, half, at(2, 1) + half),
        ],
    )
    keyval = front[:, query_width:]
    flipped = jnp.concatenate([keyval[:, HD // 2 :], keyval[:, : HD // 2]], axis=1)
    own_keyval = jnp.where(core == 0, keyval * cosine + flipped * sine, keyval).astype(jnp.bfloat16)
    other_keyval = shift(own_keyval, "c", 1)
    out_other = shift(after(out_own, own_keyval), "zh", 1)

    heads = wide // HD
    which = core.astype(jnp.int32)[None]
    context_a = attend(front, 0, heads, own_keyval, other_keyval, doc_lengths, which, cosine, sine)
    again = after(other_keyval, context_a)
    context_b = attend(front, heads, heads, own_keyval, again, doc_lengths, which, cosine, sine)
    chip_a, chip_b = shift(context_a, "zl", 1), shift(context_b, "zl", 1)

    out_other, low, high, _ = lax.optimization_barrier((out_other, out_up[0], out_down[0], chip_a))
    split = out_own.shape[0] // 2
    out_far = [(shift(low[:split], "x", 1), shift(high[split:], "x", -1))]
    out_up.append(shift(out_other, "x", 1))
    out_down.append(shift(out_other, "x", -1))
    out_far.append((shift(out_up[1][:split], "x", 1), shift(out_down[1][split:], "x", -1)))

    core_a, core_b = shift(after(context_a, chip_a), "c", 1), shift(after(context_b, chip_a), "c", 1)
    both_a, both_b = shift(chip_a, "c", 1), shift(chip_b, "c", 1)
    context_a, context_b = [context_a, core_a, chip_a, both_a], [context_b, core_b, chip_b, both_b]

    chunks = []
    contexts = [context_a, context_b]
    for dz, mine in enumerate((out_own, out_other)):
        arrays = [mine, out_up[dz], out_down[dz], *out_far[dz]]
        weights = [(0, 0, 2 * split, 0, 0), (1, 0, 2 * split, 1, 0), (2, 0, 2 * split, 3, 0)]
        weights += [(3, 0, split, 2, 0), (4, 0, split, 2, split)]
        parts = out_project(place, contexts, arrays, weights)
        contexts = contexts if len(contexts) == 1 else [parts[4]]
        total = parts[0].astype(jnp.float32)
        for by in (2, 1, 3):
            total = total + shift(parts[by], "y", by).astype(jnp.float32)
        total = total.reshape(4, -1, total.shape[1])
        group = at_zl * 2 + core
        mine = lax.dynamic_index_in_dim(total, group, 0, keepdims=False)
        theirs = [lax.dynamic_index_in_dim(total, group ^ i, 0, keepdims=False).astype(jnp.bfloat16) for i in (1, 2, 3)]
        chunks.append([mine, shift(theirs[0], "c", 1), shift(theirs[1], "zl", 1), swap_both(theirs[2])])

    share = token_count // tp_count
    own_rows = lax.dynamic_slice_in_dim(hidden_in, lax.axis_index(TP) * share, share, 0)
    return finish(place, chunks, own_rows)


def solution(mesh):
    fine = Mesh(mesh.devices.reshape(4, 2, 2, 4, 2), ("x", "zh", "zl", "y", "c"))
    rep, every = ("x", "zh"), ("x", "zh", "zl", "y", "c")
    in_specs = (P(rep, None), P(), P(every, None), P(every, None), P(None, every), P(rep, None))
    return jax.shard_map(shards, mesh=fine, in_specs=in_specs, out_specs=P(every, None), check_vma=False)
```

```python
import jax
import jax.numpy as jnp
from jax import lax
from jax.experimental import pallas as pl
from jax.experimental.pallas import tpu as pltpu
from jax.sharding import Mesh
from jax.sharding import PartitionSpec as P

H = 64
KVH = 8
HD = 128

theta_base = 1000000.0
eps_norm = 1e-06

TP = ("zl", "y", "c")
LOG2E = 1.4426950408889634
VMEM = 48 * 1024 * 1024


def shift(value, axis, by):
    size = lax.axis_size(axis)
    return lax.ppermute(value, axis, [(i, (i + by) % size) for i in range(size)])


def after(value, *earlier):
    return lax.optimization_barrier((value, *earlier))[0]


def doc_starts(lengths, count):
    places = jnp.arange(count, dtype=jnp.int32)
    ends = jnp.cumsum(lengths)
    after_end = places[:, None] >= ends[None, :]
    return jnp.sum(jnp.where(after_end, lengths[None, :], 0), axis=1)


def normalize(hidden, gain):
    count, width = hidden.shape
    block = 128

    def kernel(hidden_ref, gain_ref, out_ref):
        floats = hidden_ref[...].astype(jnp.float32)
        power = jnp.mean(floats * floats, axis=-1, keepdims=True)
        out_ref[...] = (floats * lax.rsqrt(power + eps_norm) * gain_ref[...]).astype(jnp.bfloat16)

    rows = pl.BlockSpec((block, width), lambda m: (m, 0))
    return pl.pallas_call(
        kernel,
        grid=(count // block,),
        in_specs=[rows, pl.BlockSpec((1, width), lambda m: (0, 0))],
        out_specs=rows,
        out_shape=jax.ShapeDtypeStruct((count, width), jnp.bfloat16),
        compiler_params=pltpu.CompilerParams(vmem_limit_bytes=VMEM),
        cost_estimate=pl.CostEstimate(flops=6 * count * width, bytes_accessed=4 * count * width, transcendentals=count),
    )(hidden, gain[None, :])


def project(total, normed, pieces):
    count, block = normed.shape[0], 512
    width = pieces[0][0].shape[1]
    number = len(pieces)
    steps = jnp.stack([at // rows for _, _, rows, at in pieces]).astype(jnp.int32)

    def kernel(steps_ref, *refs):
        out_ref = refs[-1]
        value = None if total is None else refs[2 * number][...]
        for i in range(number):
            term = jnp.dot(refs[i][...], refs[number + i][...], preferred_element_type=jnp.float32)
            value = term if value is None else value + term
        out_ref[...] = value

    def rows_spec(i, rows):
        return pl.BlockSpec((block, rows), lambda m, steps_ref: (m, steps_ref[i]))

    def weight_spec(rows, at_block):
        return pl.BlockSpec((rows, width), lambda m, steps_ref: (at_block, 0))

    in_specs = [rows_spec(i, rows) for i, (_, _, rows, _) in enumerate(pieces)]
    in_specs += [weight_spec(rows, at_block) for _, at_block, rows, _ in pieces]
    args = [normed] * number + [weights for weights, _, _, _ in pieces]
    out_spec = pl.BlockSpec((block, width), lambda m, steps_ref: (m, 0))
    aliases = {}
    if total is not None:
        in_specs.append(out_spec)
        args.append(total)
        aliases = {2 * number + 1: 0}
    depth = sum(rows for _, _, rows, _ in pieces)
    return pl.pallas_call(
        kernel,
        grid_spec=pltpu.PrefetchScalarGridSpec(
            num_scalar_prefetch=1, grid=(count // block,), in_specs=in_specs, out_specs=out_spec
        ),
        out_shape=jax.ShapeDtypeStruct((count, width), jnp.float32),
        input_output_aliases=aliases,
        compiler_params=pltpu.CompilerParams(vmem_limit_bytes=VMEM),
        cost_estimate=pl.CostEstimate(
            flops=2 * count * depth * width, bytes_accessed=2 * depth * (count + width), transcendentals=0
        ),
    )(steps, *args)


def attention_kernel(
    lengths_ref, core_ref, query_ref, own_ref, other_ref, cos_ref, sin_ref, out_ref, key_ref, value_ref, *, block, span
):
    count = query_ref.shape[0]
    scale = HD ** (-0.5) * LOG2E

    @pl.when((pl.program_id(0) == 0) & (core_ref[0] == 0))
    def _():
        key_ref[...], value_ref[...] = own_ref[...], other_ref[...]

    @pl.when((pl.program_id(0) == 0) & (core_ref[0] != 0))
    def _():
        key_ref[...], value_ref[...] = other_ref[...], own_ref[...]

    for number in range(count // block):
        begin = number * block
        low = max(0, begin + block - span)
        rows = query_ref[begin : begin + block, :]
        turned = rows * cos_ref[begin : begin + block, :] + pltpu.roll(rows, HD // 2, 1) * sin_ref[begin : begin + block, :]
        scores = lax.dot_general(
            turned.astype(jnp.bfloat16),
            key_ref[low : begin + block, :],
            (((1,), (1,)), ((), ())),
            preferred_element_type=jnp.float32,
        )
        width = begin + block - low
        place = begin + lax.broadcasted_iota(jnp.int32, (block, 1), 0)
        start, end = jnp.zeros((block, 1), jnp.int32), 0
        for document in range(lengths_ref.shape[1]):
            end = end + lengths_ref[0, document]
            start = jnp.where(place >= end, end, start)
        key_at = low + lax.broadcasted_iota(jnp.int32, (block, width), 1)
        allowed = (key_at >= start) & (key_at <= place)
        scores = jnp.where(allowed, scores, -1e30)
        top = jnp.max(scores, axis=-1, keepdims=True)
        weights = jnp.exp2((scores - top) * scale)
        probs = (weights / jnp.sum(weights, axis=-1, keepdims=True)).astype(jnp.bfloat16)
        blended = jnp.dot(probs, value_ref[low : begin + block, :], preferred_element_type=jnp.float32)
        out_ref[begin : begin + block, :] = blended.astype(jnp.bfloat16)


def attend(projected, first, heads, keyval, other_keyval, lengths, core, cosine, sine):
    count = projected.shape[0]
    body = lambda *refs: attention_kernel(*refs, block=256, span=768)
    whole = pl.BlockSpec((count, HD), lambda h: (0, 0))
    smem = pl.BlockSpec(memory_space=pltpu.SMEM)
    return pl.pallas_call(
        body,
        grid=(heads,),
        in_specs=[smem, smem, pl.BlockSpec((count, HD), lambda h: (0, first + h)), *[whole] * 4],
        out_specs=pl.BlockSpec((count, HD), lambda h: (0, h)),
        out_shape=jax.ShapeDtypeStruct((count, heads * HD), jnp.bfloat16),
        scratch_shapes=[pltpu.VMEM((count, HD), jnp.bfloat16)] * 2,
        compiler_params=pltpu.CompilerParams(vmem_limit_bytes=VMEM),
        cost_estimate=pl.CostEstimate(
            flops=4 * heads * count * 640 * HD, bytes_accessed=8 * count * HD * heads, transcendentals=heads * count * 640
        ),
    )(lengths, core, projected, keyval, other_keyval, cosine, sine)


def out_project(place, contexts, arrays, weights):
    joined = len(contexts) == 1
    flat = contexts if joined else [piece for stream in contexts for piece in stream]
    count, depth = flat[0].shape[0], arrays[0].shape[1]
    each, columns = 256, 1024
    per_owner = count // 8

    def kernel(place_ref, *refs):
        context_refs, array_refs = refs[: len(flat)], refs[len(flat) : len(flat) + len(arrays)]
        out_refs = refs[len(flat) + len(arrays) :]
        at_x, at_y, at_pair = place_ref[0], place_ref[1], place_ref[2]
        held = context_refs[0] if joined else out_refs[4]
        if not joined:
            pairs = flat[0].shape[1]
            for number in range(len(flat)):
                stream, other = number // 4, number % 4
                group = jnp.bitwise_xor(at_pair, other)
                lane = pl.multiple_of(group * (len(contexts) * pairs) + stream * pairs, pairs)
                for by in range(4):
                    chip = lax.rem(at_y + by, 4)
                    for zl in range(2):
                        row = pl.multiple_of(zl * 4 * per_owner + chip * per_owner, per_owner)
                        to = (by * 2 + zl) * per_owner
                        held[to : to + per_owner, pl.ds(lane, pairs)] = context_refs[number][pl.ds(row, per_owner), :]
        for array, row, rows, dx, column in weights:
            lane = pl.multiple_of(lax.rem(at_x + 4 - dx, 4) * each + column, HD)
            for by in range(4):
                term = lax.dot_general(
                    held[by * 2 * per_owner : (by + 1) * 2 * per_owner, :],
                    array_refs[array][row : row + rows, :],
                    (((1,), (1,)), ((), ())),
                    preferred_element_type=jnp.float32,
                )
                out_refs[by][:, pl.ds(lane, rows)] = term.astype(jnp.bfloat16)

    vmem = pl.BlockSpec(memory_space=pltpu.VMEM)
    out_shape = [jax.ShapeDtypeStruct((2 * per_owner, columns), jnp.bfloat16)] * 4
    if not joined:
        out_shape.append(jax.ShapeDtypeStruct((count, depth), jnp.bfloat16))
    return pl.pallas_call(
        kernel,
        in_specs=[pl.BlockSpec(memory_space=pltpu.SMEM)] + [vmem] * (len(flat) + len(arrays)),
        out_specs=[vmem] * len(out_shape),
        out_shape=out_shape,
        compiler_params=pltpu.CompilerParams(vmem_limit_bytes=VMEM),
        cost_estimate=pl.CostEstimate(
            flops=2 * count * depth * columns, bytes_accessed=2 * depth * (count + columns), transcendentals=0
        ),
    )(place, *flat, *arrays)


def finish(place, chunks, rows):
    share, width = rows.shape
    flat = [piece for chunk in chunks for piece in chunk]

    def kernel(place_ref, *refs):
        rows_ref, out_ref = refs[len(flat)], refs[-1]
        at_zh, at_pair = place_ref[3], place_ref[2]
        left = lax.broadcasted_iota(jnp.int32, (share, HD), 1) < HD // 2

        def part(dz, group, lanes):
            parts = [refs[dz * 4 + i][:, lanes].astype(jnp.float32) for i in range(4)]
            other = jnp.bitwise_xor(at_pair, group)
            low = jnp.where(other % 2 == 0, parts[0], parts[1])
            high = jnp.where(other % 2 == 0, parts[2], parts[3])
            return jnp.where(other < 2, low, high)

        for x in range(4):
            for zl in range(2):
                for pair in range(2):
                    lanes = slice(x * 256 + pair * HD, x * 256 + (pair + 1) * HD)
                    found = [[part(dz, zl * 2 + c, lanes) for c in range(2)] for dz in range(2)]
                    for zh in range(2):
                        zero, one = [jnp.where(at_zh == zh, found[0][c], found[1][c]) for c in range(2)]
                        both = (
                            jnp.where(left, zero, pltpu.roll(one, HD // 2, 1)),
                            jnp.where(left, pltpu.roll(zero, HD // 2, 1), one),
                        )
                        for i in range(2):
                            at = (x * 2 + zh) * 1024 + zl * 512 + (pair * 2 + i) * HD
                            here = rows_ref[:, at : at + HD].astype(jnp.float32)
                            out_ref[:, at : at + HD] = (here + both[i]).astype(jnp.bfloat16)

    vmem = pl.BlockSpec(memory_space=pltpu.VMEM)
    return pl.pallas_call(
        kernel,
        in_specs=[pl.BlockSpec(memory_space=pltpu.SMEM)] + [vmem] * (len(flat) + 1),
        out_specs=vmem,
        out_shape=jax.ShapeDtypeStruct((share, width), jnp.bfloat16),
        compiler_params=pltpu.CompilerParams(vmem_limit_bytes=VMEM),
    )(place, *flat, rows)


def pack_projection(w_query, w_keyval, tp_count):
    rows, wide = w_query.shape[0], w_query.shape[1] // tp_count

    def kernel(query_ref, keyval_ref, out_ref):
        for group in range(tp_count):
            to = slice(group * rows, (group + 1) * rows)
            out_ref[to, :wide] = query_ref[:, group * wide : (group + 1) * wide]
            at = (group % 2 * KVH + group // 2) * HD
            out_ref[to, wide:] = keyval_ref[:, at : at + HD]

    vmem = pl.BlockSpec(memory_space=pltpu.VMEM)
    return pl.pallas_call(
        kernel,
        in_specs=[vmem, vmem],
        out_specs=vmem,
        out_shape=jax.ShapeDtypeStruct((tp_count * rows, wide + HD), jnp.bfloat16),
        compiler_params=pltpu.CompilerParams(vmem_limit_bytes=VMEM),
    )(w_query, w_keyval)


def pack_output(turned):
    columns, rows = turned.shape[0], turned.shape[1] // 8

    def kernel(in_ref, out_ref):
        for y in range(4):
            for zl in range(2):
                at = (zl * 4 + y) * rows
                out_ref[y * columns : (y + 1) * columns, zl * rows : (zl + 1) * rows] = in_ref[:, at : at + rows]

    vmem = pl.BlockSpec(memory_space=pltpu.VMEM)
    return pl.pallas_call(
        kernel,
        in_specs=[vmem],
        out_specs=vmem,
        out_shape=jax.ShapeDtypeStruct((4 * columns, 2 * rows), jnp.bfloat16),
        compiler_params=pltpu.CompilerParams(vmem_limit_bytes=VMEM),
    )(turned)


def pick(arrays, outputs):
    def kernel(*refs):
        for out_ref, parts in zip(refs[len(arrays) :], outputs):
            to = 0
            for array, row, rows in parts:
                out_ref[to : to + rows, :] = refs[array][row : row + rows, :]
                to += rows

    vmem = pl.BlockSpec(memory_space=pltpu.VMEM)
    width = arrays[0].shape[1]
    return pl.pallas_call(
        kernel,
        in_specs=[vmem] * len(arrays),
        out_specs=[vmem] * len(outputs),
        out_shape=[jax.ShapeDtypeStruct((sum(p[2] for p in parts), width), jnp.bfloat16) for parts in outputs],
        compiler_params=pltpu.CompilerParams(vmem_limit_bytes=VMEM),
    )(*arrays)


def swap_both(value):
    return lax.ppermute(value, ("zl", "c"), [(i, 3 - i) for i in range(4)])


def shards(hidden_in, norm_gain, w_query, w_keyval, w_out, doc_lengths):
    tp_count = lax.axis_size(TP)
    token_count, width = hidden_in.shape
    core, at_y, at_zl = lax.axis_index("c"), lax.axis_index("y"), lax.axis_index("zl")
    at_x, at_zh = lax.axis_index("x"), lax.axis_index("zh")
    place = jnp.stack([at_x, at_y, at_zl * 2 + core, at_zh]).astype(jnp.int32)
    chunk = w_query.shape[0] * tp_count
    query_width = w_query.shape[1] // tp_count
    wide = query_width // 2
    half, quarter = chunk // 2, chunk // 4

    own = lax.all_to_all(pack_projection(w_query, w_keyval, tp_count), TP, split_axis=0, concat_axis=0, tiled=True)
    normed = normalize(hidden_in, norm_gain)
    starts = doc_starts(doc_lengths[0], token_count)
    positions = jnp.arange(token_count, dtype=jnp.int32) - starts
    freqs = theta_base ** (-(jnp.arange(HD // 2, dtype=jnp.float32) * 2.0 / HD))
    angles = positions.astype(jnp.float32)[:, None] * freqs[None, :]
    cosine, sine = jnp.cos(angles), jnp.sin(angles)
    cosine = jnp.concatenate([cosine, cosine], axis=1)
    sine = jnp.concatenate([-sine, sine], axis=1)
    packed = pack_output(w_out.T)
    own, normed, cosine, sine, packed = lax.optimization_barrier((own, normed, cosine, sine, packed))

    def at(dx, dz):
        return (((at_x - dx) % 4) * 2 + (at_zh - dz) % 2) * chunk

    ahead, behind, other = shift(own, "x", 1), shift(own, "x", -1), shift(own, "zh", 1)

    out_rows = lax.all_to_all(packed, "y", split_axis=0, concat_axis=0, tiled=True)

    over, far_low, far_high = pick(
        [ahead, behind], [[(0, half, half), (1, half, half)], [(0, 0, half)], [(1, half, half)]]
    )
    over, far_low, far_high = shift(over, "zh", 1), shift(far_low, "x", 1), shift(far_high, "x", -1)
    (other_low,) = pick([other], [[(0, 0, half)]])
    low_ahead, low_behind = shift(other_low, "x", 1), shift(other_low, "x", -1)
    front = project(
        None,
        normed,
        [(own, 0, chunk, at(0, 0)), (ahead, 0, chunk, at(1, 0)), (behind, 0, chunk, at(3, 0)), (other, 0, chunk, at(0, 1))],
    )
    front, far_low, far_high, low_ahead, low_behind, over = lax.optimization_barrier(
        (front, far_low, far_high, low_ahead, low_behind, over)
    )
    up_far = shift(low_ahead[:quarter], "x", 1)
    down_far = shift(low_behind[quarter:], "x", -1)
    over_far = shift(far_high, "zh", 1)
    front = project(
        front,
        normed,
        [
            (far_low, 0, half, at(2, 0)),
            (far_high, 0, half, at(2, 0) + half),
            (low_ahead, 0, half, at(1, 1)),
            (low_behind, 0, half, at(3, 1)),
            (over, 0, half, at(1, 1) + half),
            (over, 1, half, at(3, 1) + half),
        ],
    )

    out_own, front = lax.optimization_barrier((out_rows, front))
    out_other = shift(out_own, "zh", 1)

    front, up_far, down_far, over_far = lax.optimization_barrier((front, up_far, down_far, over_far))
    front = project(
        front,
        normed,
        [
            (up_far, 0, quarter, at(2, 1)),
            (down_far, 0, quarter, at(2, 1) + quarter),
            (over_far, 0, half, at(2, 1) + half),
        ],
    )
    keyval = front[:, query_width:]
    flipped = jnp.concatenate([keyval[:, HD // 2 :], keyval[:, : HD // 2]], axis=1)
    own_keyval = jnp.where(core == 0, keyval * cosine + flipped * sine, keyval).astype(jnp.bfloat16)
    other_keyval = shift(own_keyval, "c", 1)
    out_keep = after(out_own, own_keyval)
    out_up, out_down = [shift(out_keep, "x", 1)], [shift(out_keep, "x", -1)]

    heads = wide // HD
    which = core.astype(jnp.int32)[None]
    context_a = attend(front, 0, heads, own_keyval, other_keyval, doc_lengths, which, cosine, sine)
    again = after(other_keyval, context_a)
    context_b = attend(front, heads, heads, own_keyval, again, doc_lengths, which, cosine, sine)
    chip_a, chip_b = shift(context_a, "zl", 1), shift(context_b, "zl", 1)

    out_other, low, high, _ = lax.optimization_barrier((out_other, out_up[0], out_down[0], chip_a))
    split = out_own.shape[0] // 2
    out_far = [(shift(low[:split], "x", 1), shift(high[split:], "x", -1))]
    out_up.append(shift(out_other, "x", 1))
    out_down.append(shift(out_other, "x", -1))
    out_far.append((shift(out_up[1][:split], "x", 1), shift(out_down[1][split:], "x", -1)))

    core_a, core_b = shift(after(context_a, chip_a), "c", 1), shift(after(context_b, chip_a), "c", 1)
    both_a, both_b = shift(chip_a, "c", 1), shift(chip_b, "c", 1)
    context_a, context_b = [context_a, core_a, chip_a, both_a], [context_b, core_b, chip_b, both_b]

    chunks = []
    contexts = [context_a, context_b]
    for dz, mine in enumerate((out_own, out_other)):
        arrays = [mine, out_up[dz], out_down[dz], *out_far[dz]]
        weights = [(0, 0, 2 * split, 0, 0), (1, 0, 2 * split, 1, 0), (2, 0, 2 * split, 3, 0)]
        weights += [(3, 0, split, 2, 0), (4, 0, split, 2, split)]
        parts = out_project(place, contexts, arrays, weights)
        contexts = contexts if len(contexts) == 1 else [parts[4]]
        total = parts[0].astype(jnp.float32)
        for by in (2, 1, 3):
            total = total + shift(parts[by], "y", by).astype(jnp.float32)
        total = total.reshape(4, -1, total.shape[1])
        group = at_zl * 2 + core
        mine = lax.dynamic_index_in_dim(total, group, 0, keepdims=False)
        theirs = [lax.dynamic_index_in_dim(total, group ^ i, 0, keepdims=False).astype(jnp.bfloat16) for i in (1, 2, 3)]
        chunks.append([mine, shift(theirs[0], "c", 1), shift(theirs[1], "zl", 1), swap_both(theirs[2])])

    share = token_count // tp_count
    own_rows = lax.dynamic_slice_in_dim(hidden_in, lax.axis_index(TP) * share, share, 0)
    return finish(place, chunks, own_rows)


def solution(mesh):
    fine = Mesh(mesh.devices.reshape(4, 2, 2, 4, 2), ("x", "zh", "zl", "y", "c"))
    rep, every = ("x", "zh"), ("x", "zh", "zl", "y", "c")
    in_specs = (P(rep, None), P(), P(every, None), P(every, None), P(None, every), P(rep, None))
    return jax.shard_map(shards, mesh=fine, in_specs=in_specs, out_specs=P(every, None), check_vma=False)
```

```python
import jax
import jax.numpy as jnp
from jax import lax
from jax.experimental import pallas as pl
from jax.experimental.pallas import tpu as pltpu
from jax.sharding import Mesh
from jax.sharding import PartitionSpec as P

H = 64
KVH = 8
HD = 128

theta_base = 1000000.0
eps_norm = 1e-06

TP = ("zl", "y", "c")
LOG2E = 1.4426950408889634
VMEM = 48 * 1024 * 1024


def shift(value, axis, by):
    size = lax.axis_size(axis)
    return lax.ppermute(value, axis, [(i, (i + by) % size) for i in range(size)])


def after(value, *earlier):
    return lax.optimization_barrier((value, *earlier))[0]


def doc_starts(lengths, count):
    places = jnp.arange(count, dtype=jnp.int32)
    ends = jnp.cumsum(lengths)
    after_end = places[:, None] >= ends[None, :]
    return jnp.sum(jnp.where(after_end, lengths[None, :], 0), axis=1)


def normalize(hidden, gain):
    count, width = hidden.shape
    block = 128

    def kernel(hidden_ref, gain_ref, out_ref):
        floats = hidden_ref[...].astype(jnp.float32)
        power = jnp.mean(floats * floats, axis=-1, keepdims=True)
        out_ref[...] = (floats * lax.rsqrt(power + eps_norm) * gain_ref[...]).astype(jnp.bfloat16)

    rows = pl.BlockSpec((block, width), lambda m: (m, 0))
    return pl.pallas_call(
        kernel,
        grid=(count // block,),
        in_specs=[rows, pl.BlockSpec((1, width), lambda m: (0, 0))],
        out_specs=rows,
        out_shape=jax.ShapeDtypeStruct((count, width), jnp.bfloat16),
        compiler_params=pltpu.CompilerParams(vmem_limit_bytes=VMEM),
        cost_estimate=pl.CostEstimate(flops=6 * count * width, bytes_accessed=4 * count * width, transcendentals=count),
    )(hidden, gain[None, :])


def project(total, normed, pieces):
    count, block = normed.shape[0], 512
    width = pieces[0][0].shape[1]
    number = len(pieces)
    steps = jnp.stack([at // rows for _, _, rows, at in pieces]).astype(jnp.int32)

    def kernel(steps_ref, *refs):
        out_ref = refs[-1]
        value = None if total is None else refs[2 * number][...]
        for i in range(number):
            term = jnp.dot(refs[i][...], refs[number + i][...], preferred_element_type=jnp.float32)
            value = term if value is None else value + term
        out_ref[...] = value

    def rows_spec(i, rows):
        return pl.BlockSpec((block, rows), lambda m, steps_ref: (m, steps_ref[i]))

    def weight_spec(rows, at_block):
        return pl.BlockSpec((rows, width), lambda m, steps_ref: (at_block, 0))

    in_specs = [rows_spec(i, rows) for i, (_, _, rows, _) in enumerate(pieces)]
    in_specs += [weight_spec(rows, at_block) for _, at_block, rows, _ in pieces]
    args = [normed] * number + [weights for weights, _, _, _ in pieces]
    out_spec = pl.BlockSpec((block, width), lambda m, steps_ref: (m, 0))
    aliases = {}
    if total is not None:
        in_specs.append(out_spec)
        args.append(total)
        aliases = {2 * number + 1: 0}
    depth = sum(rows for _, _, rows, _ in pieces)
    return pl.pallas_call(
        kernel,
        grid_spec=pltpu.PrefetchScalarGridSpec(
            num_scalar_prefetch=1, grid=(count // block,), in_specs=in_specs, out_specs=out_spec
        ),
        out_shape=jax.ShapeDtypeStruct((count, width), jnp.float32),
        input_output_aliases=aliases,
        compiler_params=pltpu.CompilerParams(vmem_limit_bytes=VMEM),
        cost_estimate=pl.CostEstimate(
            flops=2 * count * depth * width, bytes_accessed=2 * depth * (count + width), transcendentals=0
        ),
    )(steps, *args)


def attention_kernel(
    lengths_ref, core_ref, query_ref, own_ref, other_ref, cos_ref, sin_ref, out_ref, key_ref, value_ref, *, block, span
):
    count = query_ref.shape[0]
    scale = HD ** (-0.5) * LOG2E

    @pl.when((pl.program_id(0) == 0) & (core_ref[0] == 0))
    def _():
        key_ref[...], value_ref[...] = own_ref[...], other_ref[...]

    @pl.when((pl.program_id(0) == 0) & (core_ref[0] != 0))
    def _():
        key_ref[...], value_ref[...] = other_ref[...], own_ref[...]

    for number in range(count // block):
        begin = number * block
        low = max(0, begin + block - span)
        rows = query_ref[begin : begin + block, :]
        turned = rows * cos_ref[begin : begin + block, :] + pltpu.roll(rows, HD // 2, 1) * sin_ref[begin : begin + block, :]
        scores = lax.dot_general(
            turned.astype(jnp.bfloat16),
            key_ref[low : begin + block, :],
            (((1,), (1,)), ((), ())),
            preferred_element_type=jnp.float32,
        )
        width = begin + block - low
        place = begin + lax.broadcasted_iota(jnp.int32, (block, 1), 0)
        start, end = jnp.zeros((block, 1), jnp.int32), 0
        for document in range(lengths_ref.shape[1]):
            end = end + lengths_ref[0, document]
            start = jnp.where(place >= end, end, start)
        key_at = low + lax.broadcasted_iota(jnp.int32, (block, width), 1)
        allowed = (key_at >= start) & (key_at <= place)
        scores = jnp.where(allowed, scores, -1e30)
        top = jnp.max(scores, axis=-1, keepdims=True)
        weights = jnp.exp2((scores - top) * scale)
        probs = (weights * (1.0 / jnp.sum(weights, axis=-1, keepdims=True))).astype(jnp.bfloat16)
        blended = jnp.dot(probs, value_ref[low : begin + block, :], preferred_element_type=jnp.float32)
        out_ref[begin : begin + block, :] = blended.astype(jnp.bfloat16)


def attend(projected, first, heads, keyval, other_keyval, lengths, core, cosine, sine):
    count = projected.shape[0]
    body = lambda *refs: attention_kernel(*refs, block=256, span=768)
    whole = pl.BlockSpec((count, HD), lambda h: (0, 0))
    smem = pl.BlockSpec(memory_space=pltpu.SMEM)
    return pl.pallas_call(
        body,
        grid=(heads,),
        in_specs=[smem, smem, pl.BlockSpec((count, HD), lambda h: (0, first + h)), *[whole] * 4],
        out_specs=pl.BlockSpec((count, HD), lambda h: (0, h)),
        out_shape=jax.ShapeDtypeStruct((count, heads * HD), jnp.bfloat16),
        scratch_shapes=[pltpu.VMEM((count, HD), jnp.bfloat16)] * 2,
        compiler_params=pltpu.CompilerParams(vmem_limit_bytes=VMEM),
        cost_estimate=pl.CostEstimate(
            flops=4 * heads * count * 640 * HD, bytes_accessed=8 * count * HD * heads, transcendentals=heads * count * 640
        ),
    )(lengths, core, projected, keyval, other_keyval, cosine, sine)


def out_project(place, contexts, arrays, weights):
    joined = len(contexts) == 1
    flat = contexts if joined else [piece for stream in contexts for piece in stream]
    count, depth = flat[0].shape[0], arrays[0].shape[1]
    each, columns = 256, 1024
    per_owner = count // 8

    def kernel(place_ref, *refs):
        context_refs, array_refs = refs[: len(flat)], refs[len(flat) : len(flat) + len(arrays)]
        out_refs = refs[len(flat) + len(arrays) :]
        at_x, at_y, at_pair = place_ref[0], place_ref[1], place_ref[2]
        held = context_refs[0] if joined else out_refs[4]
        if not joined:
            pairs = flat[0].shape[1]
            for number in range(len(flat)):
                stream, other = number // 4, number % 4
                group = jnp.bitwise_xor(at_pair, other)
                lane = pl.multiple_of(group * (len(contexts) * pairs) + stream * pairs, pairs)
                for by in range(4):
                    chip = lax.rem(at_y + by, 4)
                    for zl in range(2):
                        row = pl.multiple_of(zl * 4 * per_owner + chip * per_owner, per_owner)
                        to = (by * 2 + zl) * per_owner
                        held[to : to + per_owner, pl.ds(lane, pairs)] = context_refs[number][pl.ds(row, per_owner), :]
        for array, row, rows, dx, column in weights:
            lane = pl.multiple_of(lax.rem(at_x + 4 - dx, 4) * each + column, HD)
            for by in range(4):
                term = lax.dot_general(
                    held[by * 2 * per_owner : (by + 1) * 2 * per_owner, :],
                    array_refs[array][row : row + rows, :],
                    (((1,), (1,)), ((), ())),
                    preferred_element_type=jnp.float32,
                )
                out_refs[by][:, pl.ds(lane, rows)] = term.astype(jnp.bfloat16)

    vmem = pl.BlockSpec(memory_space=pltpu.VMEM)
    out_shape = [jax.ShapeDtypeStruct((2 * per_owner, columns), jnp.bfloat16)] * 4
    if not joined:
        out_shape.append(jax.ShapeDtypeStruct((count, depth), jnp.bfloat16))
    return pl.pallas_call(
        kernel,
        in_specs=[pl.BlockSpec(memory_space=pltpu.SMEM)] + [vmem] * (len(flat) + len(arrays)),
        out_specs=[vmem] * len(out_shape),
        out_shape=out_shape,
        compiler_params=pltpu.CompilerParams(vmem_limit_bytes=VMEM),
        cost_estimate=pl.CostEstimate(
            flops=2 * count * depth * columns, bytes_accessed=2 * depth * (count + columns), transcendentals=0
        ),
    )(place, *flat, *arrays)


def finish(place, chunks, rows):
    share, width = rows.shape
    flat = [piece for chunk in chunks for piece in chunk]

    def kernel(place_ref, *refs):
        rows_ref, out_ref = refs[len(flat)], refs[-1]
        at_zh, at_pair = place_ref[3], place_ref[2]
        left = lax.broadcasted_iota(jnp.int32, (share, HD), 1) < HD // 2

        def part(dz, group, lanes):
            parts = [refs[dz * 4 + i][:, lanes].astype(jnp.float32) for i in range(4)]
            other = jnp.bitwise_xor(at_pair, group)
            low = jnp.where(other % 2 == 0, parts[0], parts[1])
            high = jnp.where(other % 2 == 0, parts[2], parts[3])
            return jnp.where(other < 2, low, high)

        for x in range(4):
            for zl in range(2):
                for pair in range(2):
                    lanes = slice(x * 256 + pair * HD, x * 256 + (pair + 1) * HD)
                    found = [[part(dz, zl * 2 + c, lanes) for c in range(2)] for dz in range(2)]
                    for zh in range(2):
                        zero, one = [jnp.where(at_zh == zh, found[0][c], found[1][c]) for c in range(2)]
                        both = (
                            jnp.where(left, zero, pltpu.roll(one, HD // 2, 1)),
                            jnp.where(left, pltpu.roll(zero, HD // 2, 1), one),
                        )
                        for i in range(2):
                            at = (x * 2 + zh) * 1024 + zl * 512 + (pair * 2 + i) * HD
                            here = rows_ref[:, at : at + HD].astype(jnp.float32)
                            out_ref[:, at : at + HD] = (here + both[i]).astype(jnp.bfloat16)

    vmem = pl.BlockSpec(memory_space=pltpu.VMEM)
    return pl.pallas_call(
        kernel,
        in_specs=[pl.BlockSpec(memory_space=pltpu.SMEM)] + [vmem] * (len(flat) + 1),
        out_specs=vmem,
        out_shape=jax.ShapeDtypeStruct((share, width), jnp.bfloat16),
        compiler_params=pltpu.CompilerParams(vmem_limit_bytes=VMEM),
    )(place, *flat, rows)


def pack_projection(w_query, w_keyval, tp_count):
    rows, wide = w_query.shape[0], w_query.shape[1] // tp_count

    def kernel(query_ref, keyval_ref, out_ref):
        for group in range(tp_count):
            to = slice(group * rows, (group + 1) * rows)
            out_ref[to, :wide] = query_ref[:, group * wide : (group + 1) * wide]
            at = (group % 2 * KVH + group // 2) * HD
            out_ref[to, wide:] = keyval_ref[:, at : at + HD]

    vmem = pl.BlockSpec(memory_space=pltpu.VMEM)
    return pl.pallas_call(
        kernel,
        in_specs=[vmem, vmem],
        out_specs=vmem,
        out_shape=jax.ShapeDtypeStruct((tp_count * rows, wide + HD), jnp.bfloat16),
        compiler_params=pltpu.CompilerParams(vmem_limit_bytes=VMEM),
    )(w_query, w_keyval)


def pack_output(turned):
    columns, rows = turned.shape[0], turned.shape[1] // 8

    def kernel(in_ref, out_ref):
        for y in range(4):
            for zl in range(2):
                at = (zl * 4 + y) * rows
                out_ref[y * columns : (y + 1) * columns, zl * rows : (zl + 1) * rows] = in_ref[:, at : at + rows]

    vmem = pl.BlockSpec(memory_space=pltpu.VMEM)
    return pl.pallas_call(
        kernel,
        in_specs=[vmem],
        out_specs=vmem,
        out_shape=jax.ShapeDtypeStruct((4 * columns, 2 * rows), jnp.bfloat16),
        compiler_params=pltpu.CompilerParams(vmem_limit_bytes=VMEM),
    )(turned)


def pick(arrays, outputs):
    def kernel(*refs):
        for out_ref, parts in zip(refs[len(arrays) :], outputs):
            to = 0
            for array, row, rows in parts:
                out_ref[to : to + rows, :] = refs[array][row : row + rows, :]
                to += rows

    vmem = pl.BlockSpec(memory_space=pltpu.VMEM)
    width = arrays[0].shape[1]
    return pl.pallas_call(
        kernel,
        in_specs=[vmem] * len(arrays),
        out_specs=[vmem] * len(outputs),
        out_shape=[jax.ShapeDtypeStruct((sum(p[2] for p in parts), width), jnp.bfloat16) for parts in outputs],
        compiler_params=pltpu.CompilerParams(vmem_limit_bytes=VMEM),
    )(*arrays)


def swap_both(value):
    return lax.ppermute(value, ("zl", "c"), [(i, 3 - i) for i in range(4)])


def shards(hidden_in, norm_gain, w_query, w_keyval, w_out, doc_lengths):
    tp_count = lax.axis_size(TP)
    token_count, width = hidden_in.shape
    core, at_y, at_zl = lax.axis_index("c"), lax.axis_index("y"), lax.axis_index("zl")
    at_x, at_zh = lax.axis_index("x"), lax.axis_index("zh")
    place = jnp.stack([at_x, at_y, at_zl * 2 + core, at_zh]).astype(jnp.int32)
    chunk = w_query.shape[0] * tp_count
    query_width = w_query.shape[1] // tp_count
    wide = query_width // 2
    half, quarter = chunk // 2, chunk // 4

    own = lax.all_to_all(pack_projection(w_query, w_keyval, tp_count), TP, split_axis=0, concat_axis=0, tiled=True)
    normed = normalize(hidden_in, norm_gain)
    starts = doc_starts(doc_lengths[0], token_count)
    positions = jnp.arange(token_count, dtype=jnp.int32) - starts
    freqs = theta_base ** (-(jnp.arange(HD // 2, dtype=jnp.float32) * 2.0 / HD))
    angles = positions.astype(jnp.float32)[:, None] * freqs[None, :]
    cosine, sine = jnp.cos(angles), jnp.sin(angles)
    cosine = jnp.concatenate([cosine, cosine], axis=1)
    sine = jnp.concatenate([-sine, sine], axis=1)
    packed = pack_output(w_out.T)
    own, normed, cosine, sine, packed = lax.optimization_barrier((own, normed, cosine, sine, packed))

    def at(dx, dz):
        return (((at_x - dx) % 4) * 2 + (at_zh - dz) % 2) * chunk

    ahead, behind, other = shift(own, "x", 1), shift(own, "x", -1), shift(own, "zh", 1)

    out_rows = lax.all_to_all(packed, "y", split_axis=0, concat_axis=0, tiled=True)

    over, far_low, far_high = pick(
        [ahead, behind], [[(0, half, half), (1, half, half)], [(0, 0, half)], [(1, half, half)]]
    )
    over, far_low, far_high = shift(over, "zh", 1), shift(far_low, "x", 1), shift(far_high, "x", -1)
    (other_low,) = pick([other], [[(0, 0, half)]])
    low_ahead, low_behind = shift(other_low, "x", 1), shift(other_low, "x", -1)
    front = project(
        None,
        normed,
        [(own, 0, chunk, at(0, 0)), (ahead, 0, chunk, at(1, 0)), (behind, 0, chunk, at(3, 0)), (other, 0, chunk, at(0, 1))],
    )
    front, far_low, far_high, low_ahead, low_behind, over = lax.optimization_barrier(
        (front, far_low, far_high, low_ahead, low_behind, over)
    )
    up_far = shift(low_ahead[:quarter], "x", 1)
    down_far = shift(low_behind[quarter:], "x", -1)
    over_far = shift(far_high, "zh", 1)
    front = project(
        front,
        normed,
        [
            (far_low, 0, half, at(2, 0)),
            (far_high, 0, half, at(2, 0) + half),
            (low_ahead, 0, half, at(1, 1)),
            (low_behind, 0, half, at(3, 1)),
            (over, 0, half, at(1, 1) + half),
            (over, 1, half, at(3, 1) + half),
        ],
    )

    out_own, front = lax.optimization_barrier((out_rows, front))
    out_other = shift(out_own, "zh", 1)

    front, up_far, down_far, over_far = lax.optimization_barrier((front, up_far, down_far, over_far))
    front = project(
        front,
        normed,
        [
            (up_far, 0, quarter, at(2, 1)),
            (down_far, 0, quarter, at(2, 1) + quarter),
            (over_far, 0, half, at(2, 1) + half),
        ],
    )
    keyval = front[:, query_width:]
    flipped = jnp.concatenate([keyval[:, HD // 2 :], keyval[:, : HD // 2]], axis=1)
    own_keyval = jnp.where(core == 0, keyval * cosine + flipped * sine, keyval).astype(jnp.bfloat16)
    other_keyval = shift(own_keyval, "c", 1)
    out_keep = after(out_own, own_keyval)
    out_up, out_down = [shift(out_keep, "x", 1)], [shift(out_keep, "x", -1)]

    heads = wide // HD
    which = core.astype(jnp.int32)[None]
    context_a = attend(front, 0, heads, own_keyval, other_keyval, doc_lengths, which, cosine, sine)
    again = after(other_keyval, context_a)
    context_b = attend(front, heads, heads, own_keyval, again, doc_lengths, which, cosine, sine)
    chip_a, chip_b = shift(context_a, "zl", 1), shift(context_b, "zl", 1)

    out_other, low, high, _ = lax.optimization_barrier((out_other, out_up[0], out_down[0], chip_a))
    split = out_own.shape[0] // 2
    out_far = [(shift(low[:split], "x", 1), shift(high[split:], "x", -1))]
    out_up.append(shift(out_other, "x", 1))
    out_down.append(shift(out_other, "x", -1))
    out_far.append((shift(out_up[1][:split], "x", 1), shift(out_down[1][split:], "x", -1)))

    core_a, core_b = shift(after(context_a, chip_a), "c", 1), shift(after(context_b, chip_a), "c", 1)
    both_a, both_b = shift(chip_a, "c", 1), shift(chip_b, "c", 1)
    context_a, context_b = [context_a, core_a, chip_a, both_a], [context_b, core_b, chip_b, both_b]

    chunks = []
    contexts = [context_a, context_b]
    for dz, mine in enumerate((out_own, out_other)):
        arrays = [mine, out_up[dz], out_down[dz], *out_far[dz]]
        weights = [(0, 0, 2 * split, 0, 0), (1, 0, 2 * split, 1, 0), (2, 0, 2 * split, 3, 0)]
        weights += [(3, 0, split, 2, 0), (4, 0, split, 2, split)]
        parts = out_project(place, contexts, arrays, weights)
        contexts = contexts if len(contexts) == 1 else [parts[4]]
        total = parts[0].astype(jnp.float32)
        for by in (2, 1, 3):
            total = total + shift(parts[by], "y", by).astype(jnp.float32)
        total = total.reshape(4, -1, total.shape[1])
        group = at_zl * 2 + core
        mine = lax.dynamic_index_in_dim(total, group, 0, keepdims=False)
        theirs = [lax.dynamic_index_in_dim(total, group ^ i, 0, keepdims=False).astype(jnp.bfloat16) for i in (1, 2, 3)]
        chunks.append([mine, shift(theirs[0], "c", 1), shift(theirs[1], "zl", 1), swap_both(theirs[2])])

    share = token_count // tp_count
    own_rows = lax.dynamic_slice_in_dim(hidden_in, lax.axis_index(TP) * share, share, 0)
    return finish(place, chunks, own_rows)


def solution(mesh):
    fine = Mesh(mesh.devices.reshape(4, 2, 2, 4, 2), ("x", "zh", "zl", "y", "c"))
    rep, every = ("x", "zh"), ("x", "zh", "zl", "y", "c")
    in_specs = (P(rep, None), P(), P(every, None), P(every, None), P(None, every), P(rep, None))
    return jax.shard_map(shards, mesh=fine, in_specs=in_specs, out_specs=P(every, None), check_vma=False)
```
